512 devices in a mesh: dp: 32 (over z, core), tensor: 16 (over y, x).
Axes of the slice: x: 4, y: 4, z: 16, core: 2. Of those that a mesh axis runs over, the one named last changes fastest.
Arguments:
- attn_out: bfloat16 [8192, 8192], P('dp', 'tensor'), parts along dimension 0, may hold values from -6 to 6
- head_signs: int32 [64], replicated, may hold values from 0 to 1
- w_out: bfloat16 [8192, 8192], P('tensor'), may hold values from -0.09375 to 0.09375
- out_exp: int32 [8192], P('tensor'), may hold values from -2 to 1
- residual: bfloat16 [8192, 8192], P('dp', 'tensor'), parts along dimension 0, may hold values from -60 to 60
- norm_gain: bfloat16 [8192], P('tensor'), may hold values from 0.25 to 1.75
- w_kv: bfloat16 [8192, 2048], P(None, 'tensor'), may hold values from -0.0625 to 0.0625
- kv_exp: int32 [2048], P('tensor'), may hold values from -2 to 1
Outputs:
- resid_out: bfloat16 [8192, 8192], P('dp', 'tensor'), parts along dimension 0
- kv: bfloat16 [8192, 2048], P('dp', 'tensor'), parts along dimension 0
The draws below stay inside these ranges and needn't reach their ends.
There are 32 independent parts, one for each index of `dp`. The reference program is written for one: setup_inputs(seed, part) draws one part's arguments, and reference() takes and returns one part's arrays. A program takes and returns all parts, laid end to end along the dimension named above; an argument that names none is the same for every part. Nothing has to cross between parts.
Inputs may be any that keep to these rules, and one draw needn't show every extreme that they name: The sign of head h is 2 head_signs[h] - 1.
All inputs are finite; a program needn't handle non-finite values.
Results may differ from the reference program's by a relative error of at most 0.025.
Values may be sent and summed in bfloat16 or wider, within the bound.
A program may use at most 64 MiB of HBM per device.

```python
import jax
import jax.numpy as jnp
from jax import lax

HEADS = 64
HD = 128
D = 8192
TOK = 256
KV_COLS = 2048
N_TENSOR = 16


def draw_residual(key, part):
    key = jax.random.fold_in(key, 7)
    key_base, key_cols, key_rows = jax.random.split(key, 3)
    col_ramp = 10.0 ** (jnp.arange(D, dtype=jnp.float32) / D - 0.5)
    col_rough = jax.random.uniform(key_cols, (D,), jnp.float32, 0.6, 1.4)
    row_scale = 10.0 ** jax.random.uniform(key_rows, (TOK, 1), jnp.float32, -0.5, 0.5)
    base = jax.random.truncated_normal(key_base, -5.0, 5.0, (TOK, D), jnp.float32)
    return (0.5 * base * row_scale * col_ramp[None, :] * col_rough[None, :]).astype(jnp.bfloat16)


def touch_ends(entries, rng, low, top_value):
    longest = entries.shape.index(max(entries.shape))
    spots = []
    for shift in (0, 1):
        where = [jax.random.randint(jax.random.fold_in(rng, axis), (), 0, length) for axis, length in enumerate(entries.shape)]
        where[longest] = (where[longest] + shift) % entries.shape[longest]
        spots.append(tuple(where))
    return entries.at[spots[0]].set(low).at[spots[1]].set(top_value)


def strengthened(entries, own_key, source, target, shards_of, factor):
    owner, partner = [(jnp.arange(entries.shape[axis_at]) // (entries.shape[axis_at] // shards_of)).reshape([-1 if axis == axis_at else 1 for axis in range(entries.ndim)]) for axis_at in (source, target)]
    chosen = jax.random.permutation(own_key, shards_of)[partner]
    strong = (owner == chosen) | (owner == (partner + shards_of // 2) % shards_of)
    return jnp.where(strong, factor * entries, entries)


def shard_levels(key, dims, cuts, least, top_value):
    factor_of = 1.0
    for position, parts in cuts:
        steps = jax.random.uniform(jax.random.fold_in(jax.random.fold_in(key, 6), position), (parts,), jnp.float32, least / len(cuts), top_value / len(cuts))
        factor_of = factor_of * jnp.repeat(jnp.exp(steps), dims[position] // parts).reshape((-1,) + (1,) * (len(dims) - 1 - position))
    return factor_of


def gaussian(rng, shape, spread, bound, cuts=(), kind=jnp.bfloat16):
    loudness = shard_levels(rng, shape, cuts, -0.22, 0.18) if cuts else 1.0
    result = jax.random.normal(rng, shape, jnp.float32) * spread * loudness
    return jnp.minimum(jnp.maximum(result, -bound), bound).astype(kind)


def bell_draw_with(stream_key, dims, scale, most, shards, heavy, kind=jnp.bfloat16):
    array = scale * jax.random.normal(stream_key, dims, jnp.float32)
    if shards:
        array = array * shard_levels(stream_key, dims, shards, -0.22, 0.18)
    return jnp.clip(strengthened(array, jax.random.fold_in(stream_key, 3), *heavy), -most, most).astype(kind)


def setup_inputs(seed: int = 0, part: int = 0) -> dict:
    keys = jax.random.split(jax.random.key(seed), 9)
    part_splits = jax.random.split(jax.random.fold_in(keys[8], part), 9)
    return {
        "attn_out": gaussian(part_splits[0], (TOK, HEADS * HD), 1.0, 6.0, ((1, 16),)),
        "head_signs": touch_ends(jax.random.randint(keys[1], (HEADS,), 0, 2), jax.random.fold_in(keys[1], 1), 0, 1).astype(jnp.int32),
        "w_out": bell_draw_with(keys[2], (HEADS * HD, D), (HEADS * HD) ** -0.5, 0.09375, ((0, 16),), (0, 1, 16, 2.0)),
        "out_exp": touch_ends(jax.random.randint(keys[3], (D,), -2, 2), jax.random.fold_in(keys[3], 1), -2, 1).astype(jnp.int32),
        "residual": draw_residual(jax.random.fold_in(jax.random.fold_in(keys[8], part), 71), part),
        "norm_gain": jnp.clip(1.0 + 0.15 * jax.random.normal(keys[5], (D,), jnp.float32), 0.25, 1.75).astype(jnp.bfloat16),
        "w_kv": gaussian(keys[6], (D, KV_COLS), D ** -0.5, 0.0625, ((1, 16),)),
        "kv_exp": touch_ends(jax.random.randint(keys[7], (KV_COLS,), -2, 2), jax.random.fold_in(keys[7], 1), -2, 1).astype(jnp.int32),
    }


def sylvester(order):
    row_ids = jnp.arange(order, dtype=jnp.int32)
    parity = jnp.zeros((order, order), jnp.int32)
    for bit_level in range(order.bit_length() - 1):
        parity = parity ^ row_ids[:, None] >> bit_level & row_ids[None, :] >> bit_level & 1
    return (1 - 2 * parity).astype(jnp.float32)

def reference(attn_out, head_signs, w_out, out_exp, residual, norm_gain, w_kv, kv_exp):
    tok_rows = attn_out.shape[0]
    sign_values = (2 * head_signs - 1).astype(jnp.float32)
    signed = attn_out.astype(jnp.float32).reshape(tok_rows, HEADS, HD) * sign_values[None, :, None]
    blended = jnp.einsum('thd,hg->tgd', signed, sylvester(HEADS), precision=lax.Precision.HIGHEST)
    rotated = (blended * HEADS ** (-0.5)).astype(jnp.bfloat16).reshape(tok_rows, HEADS * HD)
    group_rows = HEADS * HD // N_TENSOR
    pieces = rotated.reshape(tok_rows, N_TENSOR, group_rows).transpose(1, 0, 2)
    weights = w_out.reshape(N_TENSOR, group_rows, D)

    def accumulate(running, operands):
        dev_term = jnp.dot(operands[0], operands[1], preferred_element_type=jnp.float32)
        rounded = lax.optimization_barrier(dev_term.astype(jnp.bfloat16))
        return (running + rounded.astype(jnp.float32), None)
    summed, _ = lax.scan(accumulate, jnp.zeros((tok_rows, D), jnp.float32), (pieces, weights))
    projected = summed * jnp.exp2(out_exp.astype(jnp.float32))[None, :]
    resid_out = (residual.astype(jnp.float32) + projected).astype(jnp.bfloat16)
    hidden_f = resid_out.astype(jnp.float32)
    mean_sq = lax.optimization_barrier(jnp.mean(hidden_f * hidden_f, axis=1))
    normed = (hidden_f * lax.rsqrt(mean_sq + 1e-05)[:, None] * norm_gain.astype(jnp.float32)[None, :]).astype(jnp.bfloat16)
    kv_acc = jnp.dot(normed, w_kv, preferred_element_type=jnp.float32)
    kv = (kv_acc * jnp.exp2(kv_exp.astype(jnp.float32))[None, :]).astype(jnp.bfloat16)
    return (resid_out, kv)
```

```python
import functools

import jax
import jax.numpy as jnp
from jax import lax
from jax.experimental import pallas as pl
from jax.experimental.pallas import tpu as pltpu
from jax.sharding import PartitionSpec as P

MESH = pl.DeviceIdType.MESH
BF16 = jnp.bfloat16
F32 = jnp.float32
HD = 128
LH = 4
N = 16
TOK = 256
BLK = 512
D = N * BLK
KVB = 128
GROUPS = 2
GR = TOK // GROUPS
HR = GR // 2
QR = HR // 2
CHUNKS = (2, 1, 3, 0)
ORDER = (
    (2, 2), (1, 2), (2, 1), (3, 2), (2, 3), (0, 2), (2, 0), (1, 1),
    (1, 3), (3, 1), (3, 3), (0, 1), (0, 3), (1, 0), (3, 0), (0, 0),
)


def hadamard(vals):
    step = 1
    while step < len(vals):
        out = list(vals)
        for i in range(len(vals)):
            if not i & step:
                out[i] = vals[i] + vals[i | step]
                out[i | step] = vals[i] - vals[i | step]
        vals = out
        step *= 2
    return vals


def kernel(
    n_dp,
    attn, signs, w_out, out_exp, residual, gain, w_kv, kv_exp,
    resid_out, kv_out,
    sgn, att, mixed, turned, rot, w, pb, s1, f, q, own, s1b, fb,
    wkv, xn, kp, kr, sqs, sqr, res, ro, gn, oe, ke, ko,
    in_sem, w_sem, out_sem,
    a_send, a_recv, k_send, k_recv, r_send, r_recv,
    p_send, s1_recv, f_recv, q_send, s1b_recv, fb_recv,
    z_send, zr_recv, zl_recv, sib_recv,
    kv_send, kv_recv, sq_send, sq_recv,
):
    me = lax.axis_index("tensor")
    dp = lax.axis_index("dp")
    y, x = me // 4, lax.rem(me, 4)
    z, core = dp // 2, lax.rem(dp, 2)
    nz = n_dp // 2
    ck = BLK // n_dp

    def at_yx(dy, dx):
        return lax.rem(y + dy, 4) * 4 + lax.rem(x + dx, 4)

    along = (
        ({"tensor": at_yx(0, 1)}, {"tensor": at_yx(0, 3)}),
        ({"tensor": at_yx(1, 0)}, {"tensor": at_yx(3, 0)}),
    )
    z_up = {"dp": lax.rem(z + 1, nz) * 2 + core}
    z_down = {"dp": lax.rem(z + nz - 1, nz) * 2 + core}
    sibling = {"dp": z * 2 + 1 - core}

    def send(src, dst, send_sem, recv_sem, to):
        pltpu.make_async_remote_copy(
            src_ref=src, dst_ref=dst, send_sem=send_sem, recv_sem=recv_sem,
            device_id=to, device_id_type=MESH,
        ).start()

    def wait(ref, sem):
        pltpu.make_async_copy(ref, ref, sem).wait()

    def to_peers(fn):
        def one(k, carry):
            fn(lax.rem(me + k, N))
            return carry

        lax.fori_loop(1, N, one, 0)

    mine = pl.ds(pl.multiple_of(me * 16, 16), 16)
    my_rows = pl.ds(pl.multiple_of(dp * ck, ck), ck)
    my_cols = pl.ds(pl.multiple_of(me * KVB, KVB), KVB)
    loads = [
        pltpu.make_async_copy(attn.at[mine, :], att.at[me], in_sem.at[0]),
        pltpu.make_async_copy(signs, sgn, in_sem.at[1]),
        pltpu.make_async_copy(
            w_kv.at[pl.ds(pl.multiple_of(me * BLK + dp * ck, ck), ck), :],
            wkv.at[my_rows, my_cols], in_sem.at[2],
        ),
        pltpu.make_async_copy(out_exp, oe, in_sem.at[3]),
        pltpu.make_async_copy(residual, res, in_sem.at[4]),
        pltpu.make_async_copy(gain, gn, in_sem.at[5]),
        pltpu.make_async_copy(kv_exp, ke, in_sem.at[6]),
    ]
    for copy in loads:
        copy.start()

    w_loads = {}
    for i, (dy, dx) in enumerate(ORDER):
        columns = pl.ds(pl.multiple_of(at_yx(dy, dx) * BLK, BLK), BLK)
        w_loads[dy, dx] = pltpu.make_async_copy(w_out.at[:, columns], w.at[dy, dx], w_sem.at[i])

    barrier = pltpu.get_barrier_semaphore()

    def greet(j):
        pl.semaphore_signal(barrier, inc=1, device_id={"tensor": j}, device_id_type=MESH)

    to_peers(greet)
    for to in (z_up, z_down, sibling):
        pl.semaphore_signal(barrier, inc=1, device_id=to, device_id_type=MESH)
    pl.semaphore_wait(barrier, N - 1 + 3)

    def send_tokens(j):
        rows = pl.ds(pl.multiple_of(j * 16, 16), 16)
        send(attn.at[rows, :], att.at[me], a_send, a_recv, {"tensor": j})

    to_peers(send_tokens)

    def send_kv_rows(j):
        rows = pl.ds(pl.multiple_of(j * BLK + dp * ck, ck), ck)
        send(w_kv.at[rows, :], wkv.at[my_rows, my_cols], k_send, k_recv, {"tensor": j})

    to_peers(send_kv_rows)
    for dy, dx in ORDER:
        w_loads[dy, dx].start()

    loads[0].wait()
    loads[1].wait()
    wait(att.at[pl.ds(0, N - 1)], a_recv)
    for s in range(N):
        heads = []
        for h in range(LH):
            sign = (2 * sgn[s * LH + h] - 1).astype(F32)
            heads.append(att[s, :, h * HD : (h + 1) * HD].astype(F32) * sign)
        for h, val in enumerate(hadamard(heads)):
            mixed[s, :, h * HD : (h + 1) * HD] = val
    for h in range(LH):
        at = slice(h * HD, (h + 1) * HD)
        for g, val in enumerate(hadamard([mixed[s, :, at] for s in range(N)])):
            turned[g, :, at] = (val * 0.125).astype(BF16)

    def send_turned(j):
        send(turned.at[j], rot.at[mine, :], r_send, r_recv, {"tensor": j})

    to_peers(send_turned)
    rot[mine, :] = turned[me]

    def z_rows(step):
        chunk = lax.rem(z + step + nz, nz) * 2 + core
        return wkv.at[pl.ds(pl.multiple_of(chunk * ck, ck), ck), :]

    def z_start():
        loads[2].wait()
        wait(wkv.at[pl.ds(0, ck), pl.ds(0, (N - 1) * KVB)], k_recv)
        part = z_rows(0)
        send(part, part, z_send, zr_recv.at[0], z_up)
        send(part, part, z_send, zl_recv.at[0], z_down)
        send(part, part, z_send, sib_recv, sibling)

    def z_step(s):
        part = z_rows(-s)
        wait(part, zr_recv.at[s - 1])
        if s < nz // 2:
            send(part, part, z_send, zr_recv.at[s], z_up)
        send(part, part, z_send, sib_recv, sibling)
        if s < nz // 2:
            part = z_rows(s)
            wait(part, zl_recv.at[s - 1])
            if s < nz // 2 - 1:
                send(part, part, z_send, zl_recv.at[s], z_down)
            send(part, part, z_send, sib_recv, sibling)

    z_todo = list(range(1, nz // 2 + 1))

    def z_next():
        if z_todo:
            z_step(z_todo.pop(0))

    def block(half, c, a):
        return (c, a) if half == 0 else (a, c)

    def row0(half, g):
        return g * GR + half * HR

    def matmul(dy, dx):
        w_loads[dy, dx].wait()
        pb[dy, dx] = jnp.dot(rot[...], w[dy, dx], preferred_element_type=F32).astype(BF16)

    def first_far(half, g, c):
        dy, dx = block(half, c, 2)
        r = row0(half, g)
        for way in range(2):
            send(
                pb.at[dy, dx, pl.ds(r + way * QR, QR), :], s1.at[half, g, c, way],
                p_send, s1_recv.at[half, g, c, way], along[half][way],
            )

    def first_near(half, g, c):
        r = row0(half, g)
        for way, a in enumerate((1, 3)):
            dy, dx = block(half, c, a)
            part = slice(r + way * QR, r + (way + 1) * QR)
            wait(s1.at[half, g, c, way], s1_recv.at[half, g, c, way])
            pb[dy, dx, part, :] = (
                pb[dy, dx, part, :].astype(F32) + s1[half, g, c, way].astype(F32)
            ).astype(BF16)
            send(
                pb.at[dy, dx, pl.ds(r, HR), :], f.at[half, g, c, way],
                p_send, f_recv.at[half, g, c, way], along[half][way],
            )

    def second(half, g, c):
        r = row0(half, g)
        dy, dx = block(half, c, 0)
        total = pb[dy, dx, r : r + HR, :].astype(F32)
        for way in range(2):
            wait(f.at[half, g, c, way], f_recv.at[half, g, c, way])
            total = total + f[half, g, c, way].astype(F32)
        if c == 0:
            own[half, g] = total
            return
        q[half, g, c - 1] = total.astype(BF16)
        if c == 2:
            for way in range(2):
                send(
                    q.at[half, g, 1, pl.ds(way * QR, QR), :], s1b.at[half, g, way],
                    q_send, s1b_recv.at[half, g, way], along[1 - half][way],
                )
            return
        way = 0 if c == 1 else 1
        part = slice(way * QR, (way + 1) * QR)
        wait(s1b.at[half, g, way], s1b_recv.at[half, g, way])
        q[half, g, c - 1, part, :] = (
            total[part, :] + s1b[half, g, way].astype(F32)
        ).astype(BF16)
        send(
            q.at[half, g, c - 1], fb.at[half, g, way],
            q_send, fb_recv.at[half, g, way], along[1 - half][way],
        )

    def residual_rows(g):
        out_scale = jnp.exp2(oe[...].astype(F32))
        gains = gn[...].astype(F32)
        squares = []
        for half in range(2):
            rows = slice(row0(half, g), row0(half, g) + HR)
            total = own[half, g]
            for way in range(2):
                wait(fb.at[half, g, way], fb_recv.at[half, g, way])
                total = total + fb[half, g, way].astype(F32)
            out = (res[rows, :].astype(F32) + total * out_scale).astype(BF16)
            ro[rows, :] = out
            hidden = out.astype(F32)
            xn[rows, :] = (hidden * gains).astype(BF16)
            squares.append(jnp.sum(hidden * hidden, axis=1, keepdims=True))
        column = jnp.concatenate(squares, axis=0)
        sqs[g] = jnp.transpose(jnp.broadcast_to(column, (GR, 128)))[:8, :]
        rows = pl.ds(g * GR, GR)
        pltpu.make_async_copy(ro.at[rows, :], resid_out.at[rows, :], out_sem.at[g]).start()

    def project(g):
        sqr[g, me] = sqs[g]

        def send_square(j):
            send(sqs.at[g], sqr.at[g, me], sq_send.at[g], sq_recv.at[g], {"tensor": j})

        to_peers(send_square)
        rows = slice(g * GR, (g + 1) * GR)
        for i in range(4):
            part = jnp.dot(
                xn[rows, :], wkv[:, i * 512 : (i + 1) * 512], preferred_element_type=F32
            ).astype(BF16)
            for k in range(4):
                kp[g, i * 4 + k] = part[:, k * KVB : (k + 1) * KVB]
        kr[g, me] = kp[g, me]

        def send_part(j):
            send(kp.at[g, j], kr.at[g, me], kv_send.at[g], kv_recv.at[g], {"tensor": j})

        to_peers(send_part)

    def finish(g):
        wait(sqr.at[g, pl.ds(0, N - 1)], sq_recv.at[g])
        total_sq = sqr[g, 0]
        for s in range(1, N):
            total_sq = total_sq + sqr[g, s]
        inv = lax.rsqrt(total_sq / D + 1e-05)
        scale = jnp.transpose(jnp.broadcast_to(inv[:1, :], (128, GR)))
        scale = scale * jnp.exp2(ke[...].astype(F32))
        wait(kr.at[g, pl.ds(0, N - 1)], kv_recv.at[g])
        total = kr[g, 0].astype(F32)
        for s in range(1, N):
            total = total + kr[g, s].astype(F32)
        ko[g * GR : (g + 1) * GR, :] = (total * scale).astype(BF16)
        rows = pl.ds(g * GR, GR)
        pltpu.make_async_copy(ko.at[rows, :], kv_out.at[rows, :], out_sem.at[GROUPS + g]).start()

    z_start()
    wait(rot.at[pl.ds(0, (N - 1) * 16), :], r_recv)

    matmul(2, 2)
    first_far(0, 0, 2)
    first_far(1, 0, 2)
    matmul(1, 2)
    first_far(0, 0, 1)
    matmul(2, 1)
    first_far(1, 0, 1)
    matmul(3, 2)
    first_far(0, 0, 3)
    matmul(2, 3)
    first_far(1, 0, 3)
    first_near(0, 0, 2)
    first_near(1, 0, 2)
    matmul(0, 2)
    first_far(0, 0, 0)
    matmul(2, 0)
    first_far(1, 0, 0)
    for dy, dx in ((1, 1), (1, 3), (3, 1), (3, 3)):
        matmul(dy, dx)
    z_next()
    for c in (1, 3):
        first_near(0, 0, c)
        first_near(1, 0, c)
    for dy, dx in ((0, 1), (0, 3), (1, 0), (3, 0)):
        matmul(dy, dx)
    first_near(0, 0, 0)
    first_near(1, 0, 0)
    matmul(0, 0)
    z_next()
    for c in CHUNKS:
        first_far(0, 1, c)
        first_far(1, 1, c)
    for i in range(3, 7):
        loads[i].wait()
    for c in CHUNKS:
        second(0, 0, c)
        second(1, 0, c)
        first_near(0, 1, c)
        first_near(1, 1, c)
        z_next()
    residual_rows(0)
    while z_todo:
        z_next()
    wait(wkv.at[pl.ds(0, BLK // 2), :], sib_recv)
    project(0)
    for c in CHUNKS:
        second(0, 1, c)
        second(1, 1, c)
    residual_rows(1)
    project(1)
    finish(0)
    finish(1)

    wait(att.at[pl.ds(0, N - 1)], a_send)
    wait(wkv.at[pl.ds(0, ck), pl.ds(0, (N - 1) * KVB)], k_send)
    wait(turned.at[pl.ds(0, N - 1)], r_send)
    wait(pb.at[pl.ds(0, 3)], p_send)
    wait(pb.at[0, pl.ds(0, 3)], q_send)
    wait(wkv.at[pl.ds(0, (nz - 1) * ck), :], z_send)
    wait(wkv.at[pl.ds(0, nz * ck), :], z_send)
    for g in range(GROUPS):
        wait(kp.at[g, pl.ds(0, N - 1)], kv_send.at[g])
        wait(sqr.at[g, pl.ds(0, N - 1)], sq_send.at[g])
        rows = pl.ds(g * GR, GR)
        pltpu.make_async_copy(ro.at[rows, :], resid_out.at[rows, :], out_sem.at[g]).wait()
        pltpu.make_async_copy(ko.at[rows, :], kv_out.at[rows, :], out_sem.at[GROUPS + g]).wait()


def body(n_dp, attn_out, head_signs, w_out, out_exp, residual, norm_gain, w_kv, kv_exp):
    vmem = pltpu.VMEM
    dma = pltpu.SemaphoreType.DMA
    half = BLK // n_dp
    nz = n_dp // 2
    scratch = [
        pltpu.SMEM((N * LH,), jnp.int32),
        vmem((N, 16, BLK), BF16),
        vmem((N, 16, BLK), F32),
        vmem((N, 16, BLK), BF16),
        vmem((TOK, BLK), BF16),
        vmem((4, 4, BLK, BLK), BF16),
        vmem((4, 4, TOK, BLK), BF16),
        vmem((2, GROUPS, 4, 2, QR, BLK), BF16),
        vmem((2, GROUPS, 4, 2, HR, BLK), BF16),
        vmem((2, GROUPS, 3, HR, BLK), BF16),
        vmem((2, GROUPS, HR, BLK), F32),
        vmem((2, GROUPS, 2, QR, BLK), BF16),
        vmem((2, GROUPS, 2, HR, BLK), BF16),
        vmem((BLK, N * KVB), BF16),
        vmem((TOK, BLK), BF16),
        vmem((GROUPS, N, GR, KVB), BF16),
        vmem((GROUPS, N, GR, KVB), BF16),
        vmem((GROUPS, 8, GR), F32),
        vmem((GROUPS, N, 8, GR), F32),
        vmem((TOK, BLK), BF16),
        vmem((TOK, BLK), BF16),
        vmem((1, BLK), BF16),
        vmem((1, BLK), jnp.int32),
        vmem((1, KVB), jnp.int32),
        vmem((TOK, KVB), BF16),
        dma((7,)),
        dma((16,)),
        dma((2 * GROUPS,)),
        dma, dma, dma, dma, dma, dma,
        dma,
        dma((2, GROUPS, 4, 2)),
        dma((2, GROUPS, 4, 2)),
        dma,
        dma((2, GROUPS, 2)),
        dma((2, GROUPS, 2)),
        dma,
        dma((nz // 2,)),
        dma((nz // 2,)),
        dma,
        dma((GROUPS,)), dma((GROUPS,)),
        dma((GROUPS,)), dma((GROUPS,)),
    ]
    anywhere = pl.BlockSpec(memory_space=pl.ANY)
    return pl.pallas_call(
        functools.partial(kernel, n_dp),
        out_shape=(
            jax.ShapeDtypeStruct((TOK, BLK), BF16),
            jax.ShapeDtypeStruct((TOK, KVB), BF16),
        ),
        in_specs=[anywhere] * 8,
        out_specs=(anywhere, anywhere),
        scratch_shapes=scratch,
        compiler_params=pltpu.CompilerParams(
            collective_id=0, has_side_effects=True, vmem_limit_bytes=48 * 1024 * 1024
        ),
    )(
        attn_out, head_signs, w_out, out_exp.reshape(1, BLK), residual,
        norm_gain.reshape(1, BLK), w_kv, kv_exp.reshape(1, KVB),
    )


def solution(mesh):
    placed = (
        P("dp", "tensor"),
        P(),
        P("tensor", None),
        P("tensor"),
        P("dp", "tensor"),
        P("tensor"),
        P(None, "tensor"),
        P("tensor"),
    )
    return jax.shard_map(
        functools.partial(body, mesh.shape["dp"]),
        mesh=mesh,
        in_specs=placed,
        out_specs=(P("dp", "tensor"), P("dp", "tensor")),
        check_vma=False,
    )
```

```python
import jax
import jax.numpy as jnp
from jax import lax
from jax.experimental import pallas as pl
from jax.experimental.pallas import tpu as pltpu
from jax.sharding import PartitionSpec as P

MESH = pl.DeviceIdType.MESH
BF16 = jnp.bfloat16
F32 = jnp.float32
HD = 128
LH = 4
N = 16
TOK = 256
BLK = 512
D = N * BLK
KVB = 128
GROUPS = ((0, 128), (128, 64), (192, 64))
SQW = 128
PLANES = 4
SHARES = 2 * PLANES
CK = BLK // SHARES
CHUNKS = (2, 1, 3, 0)
ORDER = (
    (2, 2), (1, 2), (2, 1), (3, 2), (2, 3), (0, 2), (2, 0), (1, 1),
    (1, 3), (3, 1), (3, 3), (0, 1), (0, 3), (1, 0), (3, 0), (0, 0),
)


def hadamard(vals):
    step = 1
    while step < len(vals):
        out = list(vals)
        for i in range(len(vals)):
            if not i & step:
                out[i] = vals[i] + vals[i | step]
                out[i | step] = vals[i] - vals[i | step]
        vals = out
        step *= 2
    return vals


def kernel(
    attn, signs, w_out, out_exp, residual, gain, w_kv, kv_exp,
    resid_out, kv_out,
    sgn, att, mixed, turned, rot, w, pb, s1, f, q, own, s1b, fb,
    wkv, xn, kp, kr, sqs, sqr, res, ro, gn, oe, ke, ko,
    in_sem, w_sem, out_sem,
    a_send, a_recv, k_send, k_recv, r_send, r_recv,
    p_send, s1_recv, f_recv, q_send, s1b_recv, fb_recv,
    z_send, z_recv, sib_send, sib_recv,
    kv_send, kv_recv, sq_send, sq_recv,
):
    me = lax.axis_index("tensor")
    dp = lax.axis_index("dp")
    y, x = me // 4, lax.rem(me, 4)
    z, core = dp // 2, lax.rem(dp, 2)
    plane = lax.rem(z, PLANES)
    share = core * PLANES + plane

    def at_yx(dy, dx):
        return lax.rem(y + dy, 4) * 4 + lax.rem(x + dx, 4)

    along = (
        ({"tensor": at_yx(0, 1)}, {"tensor": at_yx(0, 3)}),
        ({"tensor": at_yx(1, 0)}, {"tensor": at_yx(3, 0)}),
    )
    z_peers = [
        {"dp": (z - plane + lax.rem(plane + k, PLANES)) * 2 + core} for k in range(1, PLANES)
    ]
    sibling = {"dp": z * 2 + 1 - core}

    def send(src, dst, send_sem, recv_sem, to):
        pltpu.make_async_remote_copy(
            src_ref=src, dst_ref=dst, send_sem=send_sem, recv_sem=recv_sem,
            device_id=to, device_id_type=MESH,
        ).start()

    def wait(ref, sem):
        pltpu.make_async_copy(ref, ref, sem).wait()

    def to_peers(fn):
        def one(k, carry):
            fn(lax.rem(me + k, N))
            return carry

        lax.fori_loop(1, N, one, 0)

    mine = pl.ds(pl.multiple_of(me * 16, 16), 16)
    my_rows = pl.ds(pl.multiple_of(share * CK, CK), CK)
    my_cols = pl.ds(pl.multiple_of(me * KVB, KVB), KVB)
    loads = [
        pltpu.make_async_copy(attn.at[mine, :], att.at[me], in_sem.at[0]),
        pltpu.make_async_copy(signs, sgn, in_sem.at[1]),
        pltpu.make_async_copy(
            w_kv.at[pl.ds(pl.multiple_of(me * BLK + share * CK, CK), CK), :],
            wkv.at[my_rows, my_cols], in_sem.at[2],
        ),
        pltpu.make_async_copy(out_exp, oe, in_sem.at[3]),
        pltpu.make_async_copy(residual, res, in_sem.at[4]),
        pltpu.make_async_copy(gain, gn, in_sem.at[5]),
        pltpu.make_async_copy(kv_exp, ke, in_sem.at[6]),
    ]
    for copy in loads:
        copy.start()

    w_loads = {}
    for i, (dy, dx) in enumerate(ORDER):
        columns = pl.ds(pl.multiple_of(at_yx(dy, dx) * BLK, BLK), BLK)
        w_loads[dy, dx] = pltpu.make_async_copy(w_out.at[:, columns], w.at[dy, dx], w_sem.at[i])

    barrier = pltpu.get_barrier_semaphore()

    def greet(j):
        pl.semaphore_signal(barrier, inc=1, device_id={"tensor": j}, device_id_type=MESH)

    to_peers(greet)
    for to in (*z_peers, sibling):
        pl.semaphore_signal(barrier, inc=1, device_id=to, device_id_type=MESH)
    pl.semaphore_wait(barrier, N - 1 + PLANES)

    def send_tokens(j):
        rows = pl.ds(pl.multiple_of(j * 16, 16), 16)
        send(attn.at[rows, :], att.at[me], a_send, a_recv, {"tensor": j})

    to_peers(send_tokens)

    def send_kv_rows(j):
        rows = pl.ds(pl.multiple_of(j * BLK + share * CK, CK), CK)
        send(w_kv.at[rows, :], wkv.at[my_rows, my_cols], k_send, k_recv, {"tensor": j})

    to_peers(send_kv_rows)
    for dy, dx in ORDER:
        w_loads[dy, dx].start()

    loads[0].wait()
    loads[1].wait()
    wait(att.at[pl.ds(0, N - 1)], a_recv)
    for s in range(N):
        heads = []
        for h in range(LH):
            sign = (2 * sgn[s * LH + h] - 1).astype(F32)
            heads.append(att[s, :, h * HD : (h + 1) * HD].astype(F32) * sign)
        for h, val in enumerate(hadamard(heads)):
            mixed[s, :, h * HD : (h + 1) * HD] = val
    for h in range(LH):
        at = slice(h * HD, (h + 1) * HD)
        for g, val in enumerate(hadamard([mixed[s, :, at] for s in range(N)])):
            turned[g, :, at] = (val * 0.125).astype(BF16)

    def send_turned(j):
        send(turned.at[j], rot.at[mine, :], r_send, r_recv, {"tensor": j})

    to_peers(send_turned)
    rot[mine, :] = turned[me]

    def z_start():
        loads[2].wait()
        wait(wkv.at[pl.ds(0, CK), pl.ds(0, (N - 1) * KVB)], k_recv)
        part = wkv.at[my_rows, :]
        for to in z_peers:
            send(part, part, z_send, z_recv, to)

    def z_finish():
        wait(wkv.at[pl.ds(0, (PLANES - 1) * CK), :], z_recv)
        rows = pl.ds(pl.multiple_of(core * (BLK // 2), BLK // 2), BLK // 2)
        send(wkv.at[rows, :], wkv.at[rows, :], sib_send, sib_recv, sibling)

    def block(half, c, a):
        return (c, a) if half == 0 else (a, c)

    def half_rows(half, g):
        start, size = GROUPS[g]
        return start + half * (size // 2), size // 2

    def matmul(dy, dx):
        w_loads[dy, dx].wait()
        pb[dy, dx] = jnp.dot(rot[...], w[dy, dx], preferred_element_type=F32).astype(BF16)

    def first_far(half, g, c):
        dy, dx = block(half, c, 2)
        r, size = half_rows(half, g)
        qr, slot = size // 2, pl.ds(GROUPS[g][0] // 4, size // 2)
        for way in range(2):
            send(
                pb.at[dy, dx, pl.ds(r + way * qr, qr), :], s1.at[half, c, way, slot, :],
                p_send, s1_recv.at[half, g, c, way], along[half][way],
            )

    def first_near(half, g, c):
        r, size = half_rows(half, g)
        qr, at = size // 2, GROUPS[g][0] // 4
        slot = pl.ds(GROUPS[g][0] // 2, size)
        for way, a in enumerate((1, 3)):
            dy, dx = block(half, c, a)
            part = slice(r + way * qr, r + (way + 1) * qr)
            wait(s1.at[half, c, way, pl.ds(at, qr), :], s1_recv.at[half, g, c, way])
            pb[dy, dx, part, :] = (
                pb[dy, dx, part, :].astype(F32) + s1[half, c, way, at : at + qr, :].astype(F32)
            ).astype(BF16)
            send(
                pb.at[dy, dx, pl.ds(r, size), :], f.at[half, c, way, slot, :],
                p_send, f_recv.at[half, g, c, way], along[half][way],
            )

    def second(half, g, c):
        r, size = half_rows(half, g)
        qr, at, far = size // 2, GROUPS[g][0] // 2, GROUPS[g][0] // 4
        slot = pl.ds(at, size)
        dy, dx = block(half, c, 0)
        total = pb[dy, dx, r : r + size, :].astype(F32)
        for way in range(2):
            wait(f.at[half, c, way, slot, :], f_recv.at[half, g, c, way])
            total = total + f[half, c, way, at : at + size, :].astype(F32)
        if c == 0:
            own[half, at : at + size, :] = total
            return
        if c == 2:
            q[half, 1, at : at + size, :] = total.astype(BF16)
            for way in range(2):
                send(
                    q.at[half, 1, pl.ds(at + way * qr, qr), :], s1b.at[half, way, pl.ds(far, qr), :],
                    q_send, s1b_recv.at[half, g, way], along[1 - half][way],
                )
            return
        way = 0 if c == 1 else 1
        part = slice(way * qr, (way + 1) * qr)
        rest = slice((1 - way) * qr, (2 - way) * qr)
        q[half, c - 1, at + rest.start : at + rest.stop, :] = total[rest, :].astype(BF16)
        wait(s1b.at[half, way, pl.ds(far, qr), :], s1b_recv.at[half, g, way])
        q[half, c - 1, at + part.start : at + part.stop, :] = (
            total[part, :] + s1b[half, way, far : far + qr, :].astype(F32)
        ).astype(BF16)
        send(
            q.at[half, c - 1, slot, :], fb.at[half, way, slot, :],
            q_send, fb_recv.at[half, g, way], along[1 - half][way],
        )

    def residual_rows(g):
        start, group = GROUPS[g]
        at = start // 2
        out_scale = jnp.exp2(oe[...].astype(F32))
        gains = gn[...].astype(F32).reshape(1, BLK)
        squares = []
        for half in range(2):
            r, size = half_rows(half, g)
            rows = slice(r, r + size)
            total = own[half, at : at + size, :]
            for way in range(2):
                wait(fb.at[half, way, pl.ds(at, size), :], fb_recv.at[half, g, way])
                total = total + fb[half, way, at : at + size, :].astype(F32)
            out = (res[rows, :].astype(F32) + total * out_scale).astype(BF16)
            ro[rows, :] = out
            hidden = out.astype(F32)
            xn[rows, :] = (hidden * gains).astype(BF16)
            squares.append(jnp.sum(hidden * hidden, axis=1, keepdims=True))
        if group < SQW:
            squares.append(jnp.zeros((SQW - group, 1), F32))
        column = jnp.concatenate(squares, axis=0)
        sqs[g] = jnp.transpose(jnp.broadcast_to(column, (SQW, 128)))[:8, :]
        rows = pl.ds(start, group)
        pltpu.make_async_copy(ro.at[rows, :], resid_out.at[rows, :], out_sem.at[g]).start()

    def project(g):
        start, group = GROUPS[g]
        rows = slice(start, start + group)
        sqr[g, me] = sqs[g]

        def send_square(j):
            send(sqs.at[g], sqr.at[g, me], sq_send.at[g], sq_recv.at[g], {"tensor": j})

        to_peers(send_square)
        for i in range(4):
            part = jnp.dot(
                xn[rows, :], wkv[:, i * 512 : (i + 1) * 512], preferred_element_type=F32
            ).astype(BF16)
            for k in range(4):
                kp[i * 4 + k, rows, :] = part[:, k * KVB : (k + 1) * KVB]
        kr[me, rows, :] = kp[me, rows, :]
        slot = pl.ds(start, group)

        def send_part(j):
            send(
                kp.at[j, slot, :], kr.at[me, slot, :],
                kv_send.at[g], kv_recv.at[g], {"tensor": j},
            )

        to_peers(send_part)

    def finish(g):
        start, group = GROUPS[g]
        rows = slice(start, start + group)
        wait(sqr.at[g, pl.ds(0, N - 1)], sq_recv.at[g])
        total_sq = sqr[g, 0]
        for s in range(1, N):
            total_sq = total_sq + sqr[g, s]
        inv = lax.rsqrt(total_sq / D + 1e-05)
        scale = jnp.transpose(jnp.broadcast_to(inv[:1, :], (128, SQW)))[:group, :]
        scale = scale * jnp.exp2(ke[...].astype(F32))
        wait(kr.at[pl.ds(0, N - 1), pl.ds(start, group), :], kv_recv.at[g])
        total = kr[0, rows, :].astype(F32)
        for s in range(1, N):
            total = total + kr[s, rows, :].astype(F32)
        ko[rows, :] = (total * scale).astype(BF16)
        out = pl.ds(start, group)
        pltpu.make_async_copy(ko.at[out, :], kv_out.at[out, :], out_sem.at[len(GROUPS) + g]).start()

    z_start()
    wait(rot.at[pl.ds(0, (N - 1) * 16), :], r_recv)

    matmul(2, 2)
    first_far(0, 0, 2)
    first_far(1, 0, 2)
    matmul(1, 2)
    first_far(0, 0, 1)
    matmul(2, 1)
    first_far(1, 0, 1)
    matmul(3, 2)
    first_far(0, 0, 3)
    matmul(2, 3)
    first_far(1, 0, 3)
    first_near(0, 0, 2)
    first_near(1, 0, 2)
    matmul(0, 2)
    first_far(0, 0, 0)
    matmul(2, 0)
    first_far(1, 0, 0)
    for dy, dx in ((1, 1), (1, 3), (3, 1), (3, 3)):
        matmul(dy, dx)
    for c in (1, 3):
        first_near(0, 0, c)
        first_near(1, 0, c)
    for dy, dx in ((0, 1), (0, 3), (1, 0), (3, 0)):
        matmul(dy, dx)
    first_near(0, 0, 0)
    first_near(1, 0, 0)
    matmul(0, 0)
    for i in range(3, 7):
        loads[i].wait()
    last = len(GROUPS) - 1
    for g in range(last + 1):
        if g < last:
            for c in CHUNKS:
                first_far(0, g + 1, c)
                first_far(1, g + 1, c)
        for c in CHUNKS:
            second(0, g, c)
            second(1, g, c)
            if g < last:
                first_near(0, g + 1, c)
                first_near(1, g + 1, c)
            if g == 1 and c == 2:
                z_finish()
            if g > 0 and c == 3:
                if g == 1:
                    wait(wkv.at[pl.ds(0, BLK // 2), :], sib_recv)
                project(g - 1)
        residual_rows(g)
    project(last)
    for g in range(last + 1):
        finish(g)

    wait(att.at[pl.ds(0, N - 1)], a_send)
    wait(wkv.at[pl.ds(0, CK), pl.ds(0, (N - 1) * KVB)], k_send)
    wait(turned.at[pl.ds(0, N - 1)], r_send)
    wait(pb.at[pl.ds(0, 3)], p_send)
    wait(pb.at[0, pl.ds(0, 3)], q_send)
    wait(wkv.at[pl.ds(0, (PLANES - 1) * CK), :], z_send)
    wait(wkv.at[pl.ds(0, BLK // 2), :], sib_send)
    for g, (start, group) in enumerate(GROUPS):
        rows = pl.ds(start, group)
        wait(kp.at[pl.ds(0, N - 1), rows, :], kv_send.at[g])
        wait(sqr.at[g, pl.ds(0, N - 1)], sq_send.at[g])
        pltpu.make_async_copy(ro.at[rows, :], resid_out.at[rows, :], out_sem.at[g]).wait()
        pltpu.make_async_copy(
            ko.at[rows, :], kv_out.at[rows, :], out_sem.at[len(GROUPS) + g]
        ).wait()


def body(attn_out, head_signs, w_out, out_exp, residual, norm_gain, w_kv, kv_exp):
    vmem = pltpu.VMEM
    dma = pltpu.SemaphoreType.DMA
    groups = len(GROUPS)
    scratch = [
        pltpu.SMEM((N * LH,), jnp.int32),
        vmem((N, 16, BLK), BF16),
        vmem((N, 16, BLK), F32),
        vmem((N, 16, BLK), BF16),
        vmem((TOK, BLK), BF16),
        vmem((4, 4, BLK, BLK), BF16),
        vmem((4, 4, TOK, BLK), BF16),
        vmem((2, 4, 2, TOK // 4, BLK), BF16),
        vmem((2, 4, 2, TOK // 2, BLK), BF16),
        vmem((2, 3, TOK // 2, BLK), BF16),
        vmem((2, TOK // 2, BLK), F32),
        vmem((2, 2, TOK // 4, BLK), BF16),
        vmem((2, 2, TOK // 2, BLK), BF16),
        vmem((BLK, N * KVB), BF16),
        vmem((TOK, BLK), BF16),
        vmem((N, TOK, KVB), BF16),
        vmem((N, TOK, KVB), BF16),
        vmem((groups, 8, SQW), F32),
        vmem((groups, N, 8, SQW), F32),
        vmem((TOK, BLK), BF16),
        vmem((TOK, BLK), BF16),
        vmem((BLK,), BF16),
        vmem((1, BLK), jnp.int32),
        vmem((1, KVB), jnp.int32),
        vmem((TOK, KVB), BF16),
        dma((7,)),
        dma((16,)),
        dma((2 * groups,)),
        dma, dma, dma, dma, dma, dma,
        dma,
        dma((2, groups, 4, 2)),
        dma((2, groups, 4, 2)),
        dma,
        dma((2, groups, 2)),
        dma((2, groups, 2)),
        dma, dma, dma, dma,
        dma((groups,)), dma((groups,)),
        dma((groups,)), dma((groups,)),
    ]
    anywhere = pl.BlockSpec(memory_space=pl.ANY)
    return pl.pallas_call(
        kernel,
        out_shape=(
            jax.ShapeDtypeStruct((TOK, BLK), BF16),
            jax.ShapeDtypeStruct((TOK, KVB), BF16),
        ),
        in_specs=[anywhere] * 8,
        out_specs=(anywhere, anywhere),
        scratch_shapes=scratch,
        compiler_params=pltpu.CompilerParams(
            collective_id=0, has_side_effects=True, vmem_limit_bytes=62 * 1024 * 1024
        ),
    )(
        attn_out, head_signs, w_out, out_exp.reshape(1, BLK), residual,
        norm_gain, w_kv, kv_exp.reshape(1, KVB),
    )


def solution(mesh):
    placed = (
        P("dp", "tensor"),
        P(),
        P("tensor", None),
        P("tensor"),
        P("dp", "tensor"),
        P("tensor"),
        P(None, "tensor"),
        P("tensor"),
    )
    return jax.shard_map(
        body,
        mesh=mesh,
        in_specs=placed,
        out_specs=(P("dp", "tensor"), P("dp", "tensor")),
        check_vma=False,
    )
```

```python
import jax
import jax.numpy as jnp
from jax import lax
from jax.experimental import pallas as pl
from jax.experimental.pallas import tpu as pltpu
from jax.sharding import PartitionSpec as P

MESH = pl.DeviceIdType.MESH
BF16 = jnp.bfloat16
F32 = jnp.float32
HD = 128
LH = 4
N = 16
TOK = 256
BLK = 512
D = N * BLK
KVB = 128
HALF = TOK // 2
HCOL = BLK // 2
GROUPS = ((0, 64), (64, 32), (96, 32))
LANES = 128
PLANES = 4
SHARES = 2 * PLANES
CK = BLK // SHARES
PEERS = (
    (2, 2), (2, 1), (1, 2), (2, 3), (3, 2), (2, 0), (0, 2), (1, 1),
    (3, 3), (1, 3), (3, 1), (0, 1), (1, 0), (0, 3), (3, 0),
)
CHUNKS = (2, 1, 3, 0)
ORDER = (
    (2, 2), (1, 2), (2, 1), (3, 2), (2, 3), (0, 2), (2, 0), (1, 1),
    (1, 3), (3, 1), (3, 3), (0, 1), (0, 3), (1, 0), (3, 0), (0, 0),
)


def hadamard(vals):
    step = 1
    while step < len(vals):
        out = list(vals)
        for i in range(len(vals)):
            if not i & step:
                out[i] = vals[i] + vals[i | step]
                out[i | step] = vals[i] - vals[i | step]
        vals = out
        step *= 2
    return vals


def kernel(
    attn, signs, w_out, out_exp, residual, gain, w_kv, kv_exp,
    resid_out, kv_out,
    sgn, att, mixed, turned, rot, w, pb, s1, f, q, own, s1b, fb,
    wkv, xn, res, ro, gn, oe, ke, ko, kp, kr,
    in_sem, w_sem, out_sem,
    a_send, a_recv, k_send, k_recv, r_send, r_recv,
    p_send, s1_recv, f_recv, q_send, s1b_recv, fb_recv,
    z_send, z_recv, sib_send, sib_recv,
    kv_send, kv_recv,
):
    me = lax.axis_index("tensor")
    dp = lax.axis_index("dp")
    y, x = me // 4, lax.rem(me, 4)
    z, core = dp // 2, lax.rem(dp, 2)
    plane = lax.rem(z, PLANES)
    share = core * PLANES + plane

    def at_yx(dy, dx):
        return lax.rem(y + dy, 4) * 4 + lax.rem(x + dx, 4)

    along = (
        ({"tensor": at_yx(0, 1)}, {"tensor": at_yx(0, 3)}),
        ({"tensor": at_yx(1, 0)}, {"tensor": at_yx(3, 0)}),
    )
    z_peers = [
        {"dp": (z - plane + lax.rem(plane + k, PLANES)) * 2 + core} for k in range(1, PLANES)
    ]
    sibling = {"dp": z * 2 + 1 - core}

    def send(src, dst, send_sem, recv_sem, to):
        pltpu.make_async_remote_copy(
            src_ref=src, dst_ref=dst, send_sem=send_sem, recv_sem=recv_sem,
            device_id=to, device_id_type=MESH,
        ).start()

    def wait(ref, sem):
        pltpu.make_async_copy(ref, ref, sem).wait()

    def to_peers(fn):
        for dy, dx in PEERS:
            fn(at_yx(dy, dx))

    barrier = pltpu.get_barrier_semaphore()

    def greet(j):
        pl.semaphore_signal(barrier, inc=1, device_id={"tensor": j}, device_id_type=MESH)

    to_peers(greet)
    for to in (*z_peers, sibling):
        pl.semaphore_signal(barrier, inc=1, device_id=to, device_id_type=MESH)

    mine = pl.ds(pl.multiple_of(me * 16, 16), 16)
    my_rows = pl.ds(pl.multiple_of(share * CK, CK), CK)
    my_cols = pl.ds(pl.multiple_of(me * KVB, KVB), KVB)
    loads = [
        pltpu.make_async_copy(attn.at[mine, :], att.at[me], in_sem.at[0]),
        pltpu.make_async_copy(signs, sgn, in_sem.at[1]),
        pltpu.make_async_copy(
            w_kv.at[pl.ds(pl.multiple_of(me * BLK + share * CK, CK), CK), :],
            wkv.at[my_rows, my_cols], in_sem.at[2],
        ),
        pltpu.make_async_copy(out_exp, oe, in_sem.at[3]),
        pltpu.make_async_copy(residual, res, in_sem.at[4]),
        pltpu.make_async_copy(gain, gn, in_sem.at[5]),
        pltpu.make_async_copy(kv_exp, ke, in_sem.at[6]),
    ]
    for copy in loads:
        copy.start()

    w_loads = {}
    for i, (dy, dx) in enumerate(ORDER):
        columns = pl.ds(pl.multiple_of(at_yx(dy, dx) * BLK, BLK), BLK)
        w_loads[dy, dx] = pltpu.make_async_copy(w_out.at[:, columns], w.at[dy, dx], w_sem.at[i])

    pl.semaphore_wait(barrier, N - 1 + PLANES)

    def send_tokens(j):
        rows = pl.ds(pl.multiple_of(j * 16, 16), 16)
        send(attn.at[rows, :], att.at[me], a_send, a_recv, {"tensor": j})

    to_peers(send_tokens)

    def send_kv_rows(j):
        rows = pl.ds(pl.multiple_of(j * BLK + share * CK, CK), CK)
        send(w_kv.at[rows, :], wkv.at[my_rows, my_cols], k_send, k_recv, {"tensor": j})

    to_peers(send_kv_rows)
    for dy, dx in ORDER:
        w_loads[dy, dx].start()

    loads[0].wait()
    loads[1].wait()
    wait(att.at[pl.ds(0, N - 1)], a_recv)
    for s in range(N):
        heads = []
        for h in range(LH):
            sign = (2 * sgn[s * LH + h] - 1).astype(F32)
            heads.append(att[s, :, h * HD : (h + 1) * HD].astype(F32) * sign)
        for h, val in enumerate(hadamard(heads)):
            mixed[s, :, h * HD : (h + 1) * HD] = val
    for h in range(LH):
        at = slice(h * HD, (h + 1) * HD)
        for g, val in enumerate(hadamard([mixed[s, :, at] for s in range(N)])):
            turned[g, :, at] = (val * 0.125).astype(BF16)

    def send_turned(j):
        send(turned.at[j], rot.at[mine, :], r_send, r_recv, {"tensor": j})

    to_peers(send_turned)
    rot[mine, :] = turned[me]

    def z_start():
        loads[2].wait()
        wait(wkv.at[pl.ds(0, CK), pl.ds(0, (N - 1) * KVB)], k_recv)
        part = wkv.at[my_rows, :]
        for to in z_peers:
            send(part, part, z_send, z_recv, to)

    def z_finish():
        wait(wkv.at[pl.ds(0, (PLANES - 1) * CK), :], z_recv)
        rows = pl.ds(pl.multiple_of(core * (BLK // 2), BLK // 2), BLK // 2)
        send(wkv.at[rows, :], wkv.at[rows, :], sib_send, sib_recv, sibling)

    def block(half, c, a):
        return (c, a) if half == 0 else (a, c)

    def rows_of(half, g):
        start, size = GROUPS[g]
        return pl.ds(half * HALF + start, size)

    def matmul(dy, dx):
        w_loads[dy, dx].wait()
        pb[dy, dx] = jnp.dot(rot[...], w[dy, dx], preferred_element_type=F32).astype(BF16)

    def first_far(half, c):
        dy, dx = block(half, c, 2)
        for way in range(2):
            send(
                pb.at[dy, dx, pl.ds(half * HALF, HALF), pl.ds(way * HCOL, HCOL)],
                s1.at[half, c, way], p_send, s1_recv.at[half, c, way], along[half][way],
            )

    def first_near(half, g, c):
        start, size = GROUPS[g]
        slot, rows = pl.ds(start, size), rows_of(half, g)
        for way, a in enumerate((1, 3)):
            dy, dx = block(half, c, a)
            part = pl.ds(way * HCOL, HCOL)
            if g == 0:
                wait(s1.at[half, c, way], s1_recv.at[half, c, way])
            pb[dy, dx, rows, part] = (
                pb[dy, dx, rows, part].astype(F32) + s1[half, c, way, slot, :].astype(F32)
            ).astype(BF16)
            send(
                pb.at[dy, dx, rows, :], f.at[half, c, way, slot, :],
                p_send, f_recv.at[half, g, c, way], along[half][way],
            )

    def second(half, g, c):
        start, size = GROUPS[g]
        slot, rows = pl.ds(start, size), rows_of(half, g)
        dy, dx = block(half, c, 0)
        total = pb[dy, dx, rows, :].astype(F32)
        for way in range(2):
            wait(f.at[half, c, way, slot, :], f_recv.at[half, g, c, way])
            total = total + f[half, c, way, slot, :].astype(F32)
        if c == 0:
            own[half, slot, :] = total
            return
        if c == 2:
            q[half, 1, slot, :] = total.astype(BF16)
            for way in range(2):
                send(
                    q.at[half, 1, slot, pl.ds(way * HCOL, HCOL)], s1b.at[half, way, slot, :],
                    q_send, s1b_recv.at[half, g, way], along[1 - half][way],
                )
            return
        way = 0 if c == 1 else 1
        part = slice(way * HCOL, (way + 1) * HCOL)
        rest = slice((1 - way) * HCOL, (2 - way) * HCOL)
        q[half, c - 1, slot, rest] = total[:, rest].astype(BF16)
        wait(s1b.at[half, way, slot, :], s1b_recv.at[half, g, way])
        q[half, c - 1, slot, part] = (
            total[:, part] + s1b[half, way, slot, :].astype(F32)
        ).astype(BF16)
        send(
            q.at[half, c - 1, slot, :], fb.at[half, way, slot, :],
            q_send, fb_recv.at[half, g, way], along[1 - half][way],
        )

    def residual_rows(g):
        start, size = GROUPS[g]
        slot = pl.ds(start, size)
        out_scale = jnp.exp2(oe[...].astype(F32))
        gains = gn[...].astype(F32).reshape(1, BLK)
        squares = []
        for half in range(2):
            rows = rows_of(half, g)
            total = own[half, slot, :]
            for way in range(2):
                wait(fb.at[half, way, slot, :], fb_recv.at[half, g, way])
                total = total + fb[half, way, slot, :].astype(F32)
            out = (res[rows, :].astype(F32) + total * out_scale).astype(BF16)
            ro[rows, :] = out
            hidden = out.astype(F32)
            xn[pl.ds(2 * start + half * size, size), :] = (hidden * gains).astype(BF16)
            squares.append(jnp.sum(hidden * hidden, axis=1, keepdims=True))
            pltpu.make_async_copy(ro.at[rows, :], resid_out.at[rows, :], out_sem.at[2 * g + half]).start()
        if 2 * size < LANES:
            squares.append(jnp.zeros((LANES - 2 * size, 1), F32))
        column = jnp.concatenate(squares, axis=0)
        row = jnp.transpose(jnp.broadcast_to(column, (LANES, LANES)))[:16, :]
        high = row.astype(BF16).astype(F32)
        mid = (row - high).astype(BF16).astype(F32)
        low = row - high - mid
        index = lax.broadcasted_iota(jnp.int32, (16, LANES), 0)
        return jnp.where(index == 0, high, jnp.where(index == 1, mid, jnp.where(index == 2, low, 0.0)))

    def project(g, squares):
        start, size = GROUPS[g]
        squares = squares.astype(BF16)
        hidden = xn[pl.ds(2 * start, 2 * size), :]
        for i in CHUNKS:
            yy = lax.rem(y + i, 4)
            columns = pl.ds(pl.multiple_of(yy * 4 * KVB, 4 * KVB), 4 * KVB)
            part = jnp.dot(hidden, wkv[:, columns], preferred_element_type=F32).astype(BF16)
            for k in range(4):
                kp[g][yy * 4 + k, : 2 * size, :] = part[:, k * KVB : (k + 1) * KVB]
                kp[g][yy * 4 + k, 2 * size :, :] = squares
            for k in CHUNKS:
                if i or k:
                    j = at_yx(i, k)
                    send(kp[g].at[j], kr[g].at[me], kv_send.at[g], kv_recv.at[g], {"tensor": j})
        kr[g][me] = kp[g][me]

    def finish(g):
        start, size = GROUPS[g]
        wait(kr[g].at[pl.ds(0, N - 1)], kv_recv.at[g])
        total = kr[g][0].astype(F32)
        for s in range(1, N):
            total = total + kr[g][s].astype(F32)
        at = 2 * size
        total_sq = total[at : at + 1, :] + total[at + 1 : at + 2, :] + total[at + 2 : at + 3, :]
        inv = lax.rsqrt(total_sq / D + 1e-05)
        scale = jnp.transpose(jnp.broadcast_to(inv, (LANES, LANES)))[:at, :]
        out = (total[:at, :] * scale * jnp.exp2(ke[...].astype(F32))).astype(BF16)
        for half in range(2):
            rows = rows_of(half, g)
            ko[rows, :] = out[half * size : (half + 1) * size, :]
            pltpu.make_async_copy(
                ko.at[rows, :], kv_out.at[rows, :], out_sem.at[2 * (len(GROUPS) + g) + half]
            ).start()

    z_start()
    wait(rot.at[pl.ds(0, (N - 1) * 16), :], r_recv)

    for i, (dy, dx) in enumerate(ORDER):
        matmul(dy, dx)
        if dx == 2:
            first_far(0, dy)
        if dy == 2:
            first_far(1, dx)
        for c in {6: (2,), 10: (1, 3), 14: (0,)}.get(i, ()):
            first_near(0, 0, c)
            first_near(1, 0, c)
    for i in range(3, 7):
        loads[i].wait()
    last = len(GROUPS) - 1
    squares = [None] * len(GROUPS)
    for g in range(last + 1):
        for c in CHUNKS:
            second(0, g, c)
            second(1, g, c)
            if g < last:
                first_near(0, g + 1, c)
                first_near(1, g + 1, c)
            if g == 1 and c == 2:
                z_finish()
            if g > 0 and c == 3:
                if g == 1:
                    wait(wkv.at[pl.ds(0, BLK // 2), :], sib_recv)
                project(g - 1, squares[g - 1])
        squares[g] = residual_rows(g)
    project(last, squares[last])
    for g in range(last + 1):
        finish(g)

    wait(att.at[pl.ds(0, N - 1)], a_send)
    wait(wkv.at[pl.ds(0, CK), pl.ds(0, (N - 1) * KVB)], k_send)
    wait(turned.at[pl.ds(0, N - 1)], r_send)
    wait(pb.at[pl.ds(0, 3)], p_send)
    wait(pb.at[0, pl.ds(0, 3)], q_send)
    wait(wkv.at[pl.ds(0, (PLANES - 1) * CK), :], z_send)
    wait(wkv.at[pl.ds(0, BLK // 2), :], sib_send)
    for g in range(last + 1):
        wait(kp[g].at[pl.ds(0, N - 1)], kv_send.at[g])
        for half in range(2):
            rows = rows_of(half, g)
            pltpu.make_async_copy(ro.at[rows, :], resid_out.at[rows, :], out_sem.at[2 * g + half]).wait()
            pltpu.make_async_copy(
                ko.at[rows, :], kv_out.at[rows, :], out_sem.at[2 * (len(GROUPS) + g) + half]
            ).wait()


def body(attn_out, head_signs, w_out, out_exp, residual, norm_gain, w_kv, kv_exp):
    vmem = pltpu.VMEM
    dma = pltpu.SemaphoreType.DMA
    groups = len(GROUPS)
    scratch = [
        pltpu.SMEM((N * LH,), jnp.int32),
        vmem((N, 16, BLK), BF16),
        vmem((N, 16, BLK), F32),
        vmem((N, 16, BLK), BF16),
        vmem((TOK, BLK), BF16),
        vmem((4, 4, BLK, BLK), BF16),
        vmem((4, 4, TOK, BLK), BF16),
        vmem((2, 4, 2, HALF, HCOL), BF16),
        vmem((2, 4, 2, HALF, BLK), BF16),
        vmem((2, 3, HALF, BLK), BF16),
        vmem((2, HALF, BLK), F32),
        vmem((2, 2, HALF, HCOL), BF16),
        vmem((2, 2, HALF, BLK), BF16),
        vmem((BLK, N * KVB), BF16),
        vmem((TOK, BLK), BF16),
        vmem((TOK, BLK), BF16),
        vmem((TOK, BLK), BF16),
        vmem((BLK,), BF16),
        vmem((1, BLK), jnp.int32),
        vmem((1, KVB), jnp.int32),
        vmem((TOK, KVB), BF16),
        [vmem((N, 2 * size + 16, KVB), BF16) for _, size in GROUPS],
        [vmem((N, 2 * size + 16, KVB), BF16) for _, size in GROUPS],
        dma((7,)),
        dma((16,)),
        dma((4 * groups,)),
        dma, dma, dma, dma, dma, dma,
        dma,
        dma((2, 4, 2)),
        dma((2, groups, 4, 2)),
        dma,
        dma((2, groups, 2)),
        dma((2, groups, 2)),
        dma, dma, dma, dma,
        dma((groups,)), dma((groups,)),
    ]
    anywhere = pl.BlockSpec(memory_space=pl.ANY)
    return pl.pallas_call(
        kernel,
        out_shape=(
            jax.ShapeDtypeStruct((TOK, BLK), BF16),
            jax.ShapeDtypeStruct((TOK, KVB), BF16),
        ),
        in_specs=[anywhere] * 8,
        out_specs=(anywhere, anywhere),
        scratch_shapes=scratch,
        compiler_params=pltpu.CompilerParams(
            collective_id=0, has_side_effects=True, vmem_limit_bytes=62 * 1024 * 1024
        ),
    )(
        attn_out, head_signs, w_out, out_exp.reshape(1, BLK), residual,
        norm_gain, w_kv, kv_exp.reshape(1, KVB),
    )


def solution(mesh):
    placed = (
        P("dp", "tensor"),
        P(),
        P("tensor", None),
        P("tensor"),
        P("dp", "tensor"),
        P("tensor"),
        P(None, "tensor"),
        P("tensor"),
    )
    return jax.shard_map(
        body,
        mesh=mesh,
        in_specs=placed,
        out_specs=(P("dp", "tensor"), P("dp", "tensor")),
        check_vma=False,
    )
```

```python
import jax
import jax.numpy as jnp
from jax import lax
from jax.experimental import pallas as pl
from jax.experimental.pallas import tpu as pltpu
from jax.sharding import PartitionSpec as P

MESH = pl.DeviceIdType.MESH
BF16 = jnp.bfloat16
F32 = jnp.float32
HD = 128
LH = 4
N = 16
TOK = 256
BLK = 512
D = N * BLK
KVB = 128
HALF = TOK // 2
HCOL = BLK // 2
GROUPS = ((0, 64), (64, 32), (96, 32))
LANES = 128
PLANES = 4
SHARES = 2 * PLANES
CK = BLK // SHARES
PEERS = (
    (2, 2), (2, 1), (1, 2), (2, 3), (3, 2), (2, 0), (0, 2), (1, 1),
    (3, 3), (1, 3), (3, 1), (0, 1), (1, 0), (0, 3), (3, 0),
)
CHUNKS = (2, 1, 3, 0)
ORDER = (
    (2, 2), (1, 2), (2, 1), (3, 2), (2, 3), (0, 2), (2, 0), (1, 1),
    (1, 3), (3, 1), (3, 3), (0, 1), (0, 3), (1, 0), (3, 0), (0, 0),
)


def hadamard(vals):
    step = 1
    while step < len(vals):
        out = list(vals)
        for i in range(len(vals)):
            if not i & step:
                out[i] = vals[i] + vals[i | step]
                out[i | step] = vals[i] - vals[i | step]
        vals = out
        step *= 2
    return vals


def kernel(
    attn, signs, w_out, out_exp, residual, gain, w_kv, kv_exp,
    resid_out, kv_out,
    sgn, att, mixed, turned, rot, w, pb, s1, f, q, own, fb,
    wkv, xn, res, ro, gn, oe, ke, ko, kp, kr,
    in_sem, w_sem, out_sem,
    a_send, a_recv, k_send, k_recv, r_send, r_recv,
    p_send, s1_recv, f_recv, q_send, fb_recv,
    z_send, z_recv, sib_send, sib_recv,
    kv_send, kv_recv,
):
    me = lax.axis_index("tensor")
    dp = lax.axis_index("dp")
    y, x = me // 4, lax.rem(me, 4)
    z, core = dp // 2, lax.rem(dp, 2)
    nz = lax.axis_size("dp") // 2
    share = core * PLANES + lax.rem(z, PLANES)

    def at_yx(dy, dx):
        return lax.rem(y + dy, 4) * 4 + lax.rem(x + dx, 4)

    along = (
        ({"tensor": at_yx(0, 1)}, {"tensor": at_yx(0, 3)}),
        ({"tensor": at_yx(1, 0)}, {"tensor": at_yx(3, 0)}),
    )

    def at_z(k):
        return {"dp": lax.rem(z + k + nz, nz) * 2 + core}

    sibling = {"dp": z * 2 + 1 - core}

    def send(src, dst, send_sem, recv_sem, to):
        pltpu.make_async_remote_copy(
            src_ref=src, dst_ref=dst, send_sem=send_sem, recv_sem=recv_sem,
            device_id=to, device_id_type=MESH,
        ).start()

    def wait(ref, sem):
        pltpu.make_async_copy(ref, ref, sem).wait()

    def to_peers(fn):
        for dy, dx in PEERS:
            fn(at_yx(dy, dx))

    barrier = pltpu.get_barrier_semaphore()

    def greet(j):
        pl.semaphore_signal(barrier, inc=1, device_id={"tensor": j}, device_id_type=MESH)

    to_peers(greet)
    for to in (at_z(1), at_z(-1), at_z(2), at_z(-2), sibling):
        pl.semaphore_signal(barrier, inc=1, device_id=to, device_id_type=MESH)

    mine = pl.ds(pl.multiple_of(me * 16, 16), 16)
    my_rows = pl.ds(pl.multiple_of(share * CK, CK), CK)
    my_cols = pl.ds(pl.multiple_of(me * KVB, KVB), KVB)
    loads = [
        pltpu.make_async_copy(attn.at[mine, :], att.at[me], in_sem.at[0]),
        pltpu.make_async_copy(signs, sgn, in_sem.at[1]),
        pltpu.make_async_copy(
            w_kv.at[pl.ds(pl.multiple_of(me * BLK + share * CK, CK), CK), :],
            wkv.at[my_rows, my_cols], in_sem.at[2],
        ),
        pltpu.make_async_copy(out_exp, oe, in_sem.at[3]),
        pltpu.make_async_copy(residual, res, in_sem.at[4]),
        pltpu.make_async_copy(gain, gn, in_sem.at[5]),
        pltpu.make_async_copy(kv_exp, ke, in_sem.at[6]),
    ]
    for copy in loads:
        copy.start()

    w_loads = {}
    for i, (dy, dx) in enumerate(ORDER):
        columns = pl.ds(pl.multiple_of(at_yx(dy, dx) * BLK, BLK), BLK)
        w_loads[dy, dx] = pltpu.make_async_copy(w_out.at[:, columns], w.at[dy, dx], w_sem.at[i])

    pl.semaphore_wait(barrier, N - 1 + 5)

    def send_tokens(j):
        rows = pl.ds(pl.multiple_of(j * 16, 16), 16)
        send(attn.at[rows, :], att.at[me], a_send, a_recv, {"tensor": j})

    to_peers(send_tokens)

    def send_kv_rows(j):
        rows = pl.ds(pl.multiple_of(j * BLK + share * CK, CK), CK)
        send(w_kv.at[rows, :], wkv.at[my_rows, my_cols], k_send, k_recv, {"tensor": j})

    to_peers(send_kv_rows)
    for dy, dx in ORDER:
        w_loads[dy, dx].start()

    loads[0].wait()
    loads[1].wait()
    wait(att.at[pl.ds(0, N - 1)], a_recv)
    for s in range(N):
        heads = []
        for h in range(LH):
            sign = (2 * sgn[s * LH + h] - 1).astype(F32)
            heads.append(att[s, :, h * HD : (h + 1) * HD].astype(F32) * sign)
        for h, val in enumerate(hadamard(heads)):
            mixed[s, :, h * HD : (h + 1) * HD] = val
    for h in range(LH):
        at = slice(h * HD, (h + 1) * HD)
        for g, val in enumerate(hadamard([mixed[s, :, at] for s in range(N)])):
            turned[g, :, at] = (val * 0.125).astype(BF16)

    def send_turned(j):
        send(turned.at[j], rot.at[mine, :], r_send, r_recv, {"tensor": j})

    to_peers(send_turned)
    rot[mine, :] = turned[me]

    def z_start():
        loads[2].wait()
        wait(wkv.at[pl.ds(0, CK), pl.ds(0, (N - 1) * KVB)], k_recv)
        part = wkv.at[my_rows, :]
        for k in (1, -1):
            send(part, part, z_send, z_recv, at_z(k))
        for i, k in enumerate((2, -2)):
            rows = pl.ds(pl.multiple_of(share * CK + i * (CK // 2), CK // 2), CK // 2)
            send(wkv.at[rows, :], wkv.at[rows, :], z_send, z_recv, at_z(k))

    def z_finish():
        wait(wkv.at[pl.ds(0, (PLANES - 1) * CK), :], z_recv)
        rows = pl.ds(pl.multiple_of(core * (BLK // 2), BLK // 2), BLK // 2)
        send(wkv.at[rows, :], wkv.at[rows, :], sib_send, sib_recv, sibling)

    def block(half, c, a):
        return (c, a) if half == 0 else (a, c)

    def rows_of(half, g):
        start, size = GROUPS[g]
        return pl.ds(half * HALF + start, size)

    def matmul(dy, dx):
        w_loads[dy, dx].wait()
        pb[dy, dx] = jnp.dot(rot[...], w[dy, dx], preferred_element_type=F32).astype(BF16)

    def first_far(half, c):
        dy, dx = block(half, c, 2)
        for way in range(2):
            send(
                pb.at[dy, dx, pl.ds(half * HALF, HALF), pl.ds(way * HCOL, HCOL)],
                s1.at[half, c, way], p_send, s1_recv.at[half, c, way], along[half][way],
            )

    def first_near(half, g, c):
        start, size = GROUPS[g]
        slot, rows = pl.ds(start, size), rows_of(half, g)
        for way, a in enumerate((1, 3)):
            dy, dx = block(half, c, a)
            part = pl.ds(way * HCOL, HCOL)
            if g == 0:
                wait(s1.at[half, c, way], s1_recv.at[half, c, way])
            pb[dy, dx, rows, part] = (
                pb[dy, dx, rows, part].astype(F32) + s1[half, c, way, slot, :].astype(F32)
            ).astype(BF16)
            send(
                pb.at[dy, dx, rows, :], f.at[half, c, way, slot, :],
                p_send, f_recv.at[half, g, c, way], along[half][way],
            )

    def second(half, g, c):
        start, size = GROUPS[g]
        slot, rows = pl.ds(start, size), rows_of(half, g)
        dy, dx = block(half, c, 0)
        total = pb[dy, dx, rows, :].astype(F32)
        for way in range(2):
            wait(f.at[half, c, way, slot, :], f_recv.at[half, g, c, way])
            total = total + f[half, c, way, slot, :].astype(F32)
        if c == 0:
            own[half, slot, :] = total
            return
        q[half, c - 1, slot, :] = total.astype(BF16)
        to = at_yx(c, 0) if half == 0 else at_yx(0, c)
        send(
            q.at[half, c - 1, slot, :], fb.at[half, c - 1, slot, :],
            q_send, fb_recv.at[half, g, c - 1], {"tensor": to},
        )

    def residual_rows(g):
        start, size = GROUPS[g]
        slot = pl.ds(start, size)
        out_scale = jnp.exp2(oe[...].astype(F32))
        gains = gn[...].astype(F32).reshape(1, BLK)
        squares = []
        for half in range(2):
            rows = rows_of(half, g)
            total = own[half, slot, :]
            for k in range(3):
                wait(fb.at[half, k, slot, :], fb_recv.at[half, g, k])
                total = total + fb[half, k, slot, :].astype(F32)
            out = (res[rows, :].astype(F32) + total * out_scale).astype(BF16)
            ro[rows, :] = out
            hidden = out.astype(F32)
            xn[pl.ds(2 * start + half * size, size), :] = (hidden * gains).astype(BF16)
            squares.append(jnp.sum(hidden * hidden, axis=1, keepdims=True))
            pltpu.make_async_copy(ro.at[rows, :], resid_out.at[rows, :], out_sem.at[2 * g + half]).start()
        if 2 * size < LANES:
            squares.append(jnp.zeros((LANES - 2 * size, 1), F32))
        column = jnp.concatenate(squares, axis=0)
        row = jnp.transpose(jnp.broadcast_to(column, (LANES, LANES)))[:16, :]
        high = row.astype(BF16).astype(F32)
        mid = (row - high).astype(BF16).astype(F32)
        low = row - high - mid
        index = lax.broadcasted_iota(jnp.int32, (16, LANES), 0)
        return jnp.where(index == 0, high, jnp.where(index == 1, mid, jnp.where(index == 2, low, 0.0)))

    def project(g, squares):
        start, size = GROUPS[g]
        squares = squares.astype(BF16)
        hidden = xn[pl.ds(2 * start, 2 * size), :]
        for i in CHUNKS:
            yy = lax.rem(y + i, 4)
            columns = pl.ds(pl.multiple_of(yy * 4 * KVB, 4 * KVB), 4 * KVB)
            part = jnp.dot(hidden, wkv[:, columns], preferred_element_type=F32).astype(BF16)
            for k in range(4):
                kp[g][yy * 4 + k, : 2 * size, :] = part[:, k * KVB : (k + 1) * KVB]
                kp[g][yy * 4 + k, 2 * size :, :] = squares
            for k in CHUNKS:
                if i or k:
                    j = at_yx(i, k)
                    send(kp[g].at[j], kr[g].at[me], kv_send.at[g], kv_recv.at[g], {"tensor": j})
        kr[g][me] = kp[g][me]

    def finish(g):
        start, size = GROUPS[g]
        wait(kr[g].at[pl.ds(0, N - 1)], kv_recv.at[g])
        total = kr[g][0].astype(F32)
        for s in range(1, N):
            total = total + kr[g][s].astype(F32)
        at = 2 * size
        total_sq = total[at : at + 1, :] + total[at + 1 : at + 2, :] + total[at + 2 : at + 3, :]
        inv = lax.rsqrt(total_sq / D + 1e-05)
        scale = jnp.transpose(jnp.broadcast_to(inv, (LANES, LANES)))[:at, :]
        out = (total[:at, :] * scale * jnp.exp2(ke[...].astype(F32))).astype(BF16)
        for half in range(2):
            rows = rows_of(half, g)
            ko[rows, :] = out[half * size : (half + 1) * size, :]
            pltpu.make_async_copy(
                ko.at[rows, :], kv_out.at[rows, :], out_sem.at[2 * (len(GROUPS) + g) + half]
            ).start()

    z_start()
    wait(rot.at[pl.ds(0, (N - 1) * 16), :], r_recv)

    for i, (dy, dx) in enumerate(ORDER):
        matmul(dy, dx)
        if dx == 2:
            first_far(0, dy)
        if dy == 2:
            first_far(1, dx)
        for c in {6: (2,), 10: (1, 3), 14: (0,)}.get(i, ()):
            first_near(0, 0, c)
            first_near(1, 0, c)
    for i in range(3, 7):
        loads[i].wait()
    last = len(GROUPS) - 1
    squares = [None] * len(GROUPS)
    for c in CHUNKS:
        first_near(0, 1, c)
        first_near(1, 1, c)
    for g in range(last + 1):
        for i, c in enumerate(CHUNKS):
            second(0, g, c)
            second(1, g, c)
            if g + 2 <= last:
                first_near(0, g + 2, c)
                first_near(1, g + 2, c)
            if g > 0 and i == 0:
                squares[g - 1] = residual_rows(g - 1)
                if g == 1:
                    z_finish()
            if g > 0 and i == 2:
                if g == 1:
                    wait(wkv.at[pl.ds(0, BLK // 2), :], sib_recv)
                project(g - 1, squares[g - 1])
    squares[last] = residual_rows(last)
    project(last, squares[last])
    for g in range(last + 1):
        finish(g)

    wait(att.at[pl.ds(0, N - 1)], a_send)
    wait(wkv.at[pl.ds(0, CK), pl.ds(0, (N - 1) * KVB)], k_send)
    wait(turned.at[pl.ds(0, N - 1)], r_send)
    wait(pb.at[pl.ds(0, 3)], p_send)
    wait(pb.at[0, pl.ds(0, 3)], q_send)
    wait(wkv.at[pl.ds(0, (PLANES - 1) * CK), :], z_send)
    wait(wkv.at[pl.ds(0, BLK // 2), :], sib_send)
    for g in range(last + 1):
        wait(kp[g].at[pl.ds(0, N - 1)], kv_send.at[g])
        for half in range(2):
            rows = rows_of(half, g)
            pltpu.make_async_copy(ro.at[rows, :], resid_out.at[rows, :], out_sem.at[2 * g + half]).wait()
            pltpu.make_async_copy(
                ko.at[rows, :], kv_out.at[rows, :], out_sem.at[2 * (len(GROUPS) + g) + half]
            ).wait()


def body(attn_out, head_signs, w_out, out_exp, residual, norm_gain, w_kv, kv_exp):
    vmem = pltpu.VMEM
    dma = pltpu.SemaphoreType.DMA
    groups = len(GROUPS)
    scratch = [
        pltpu.SMEM((N * LH,), jnp.int32),
        vmem((N, 16, BLK), BF16),
        vmem((N, 16, BLK), F32),
        vmem((N, 16, BLK), BF16),
        vmem((TOK, BLK), BF16),
        vmem((4, 4, BLK, BLK), BF16),
        vmem((4, 4, TOK, BLK), BF16),
        vmem((2, 4, 2, HALF, HCOL), BF16),
        vmem((2, 4, 2, HALF, BLK), BF16),
        vmem((2, 3, HALF, BLK), BF16),
        vmem((2, HALF, BLK), F32),
        vmem((2, 3, HALF, BLK), BF16),
        vmem((BLK, N * KVB), BF16),
        vmem((TOK, BLK), BF16),
        vmem((TOK, BLK), BF16),
        vmem((TOK, BLK), BF16),
        vmem((BLK,), BF16),
        vmem((1, BLK), jnp.int32),
        vmem((1, KVB), jnp.int32),
        vmem((TOK, KVB), BF16),
        [vmem((N, 2 * size + 16, KVB), BF16) for _, size in GROUPS],
        [vmem((N, 2 * size + 16, KVB), BF16) for _, size in GROUPS],
        dma((7,)),
        dma((16,)),
        dma((4 * groups,)),
        dma, dma, dma, dma, dma, dma,
        dma,
        dma((2, 4, 2)),
        dma((2, groups, 4, 2)),
        dma,
        dma((2, groups, 3)),
        dma, dma, dma, dma,
        dma((groups,)), dma((groups,)),
    ]
    anywhere = pl.BlockSpec(memory_space=pl.ANY)
    return pl.pallas_call(
        kernel,
        out_shape=(
            jax.ShapeDtypeStruct((TOK, BLK), BF16),
            jax.ShapeDtypeStruct((TOK, KVB), BF16),
        ),
        in_specs=[anywhere] * 8,
        out_specs=(anywhere, anywhere),
        scratch_shapes=scratch,
        compiler_params=pltpu.CompilerParams(
            collective_id=0, has_side_effects=True, vmem_limit_bytes=62 * 1024 * 1024
        ),
    )(
        attn_out, head_signs, w_out, out_exp.reshape(1, BLK), residual,
        norm_gain, w_kv, kv_exp.reshape(1, KVB),
    )


def solution(mesh):
    placed = (
        P("dp", "tensor"),
        P(),
        P("tensor", None),
        P("tensor"),
        P("dp", "tensor"),
        P("tensor"),
        P(None, "tensor"),
        P("tensor"),
    )
    return jax.shard_map(
        body,
        mesh=mesh,
        in_specs=placed,
        out_specs=(P("dp", "tensor"), P("dp", "tensor")),
        check_vma=False,
    )
```

```python
import jax
import jax.numpy as jnp
from jax import lax
from jax.experimental import pallas as pl
from jax.experimental.pallas import tpu as pltpu
from jax.sharding import PartitionSpec as P

MESH = pl.DeviceIdType.MESH
BF16 = jnp.bfloat16
F32 = jnp.float32
HD = 128
LH = 4
N = 16
TOK = 256
BLK = 512
D = N * BLK
KVB = 128
HALF = TOK // 2
HCOL = BLK // 2
HROW = HALF // 2
LANES = 128
PLANES = 4
SHARES = 2 * PLANES
CK = BLK // SHARES
PEERS = (
    (2, 2), (2, 1), (1, 2), (2, 3), (3, 2), (2, 0), (0, 2), (1, 1),
    (3, 3), (1, 3), (3, 1), (0, 1), (1, 0), (0, 3), (3, 0),
)
CHUNKS = (2, 1, 3, 0)
ORDER = (
    (2, 2), (1, 2), (2, 1), (3, 2), (2, 3), (0, 2), (2, 0), (1, 1),
    (1, 3), (3, 1), (3, 3), (0, 1), (0, 3), (1, 0), (3, 0), (0, 0),
)


def hadamard(vals):
    step = 1
    while step < len(vals):
        out = list(vals)
        for i in range(len(vals)):
            if not i & step:
                out[i] = vals[i] + vals[i | step]
                out[i | step] = vals[i] - vals[i | step]
        vals = out
        step *= 2
    return vals


def kernel(
    attn, signs, w_out, out_exp, residual, gain, w_kv, kv_exp,
    resid_out, kv_out,
    sgn, att, mixed, turned, rot, w, pb, s1, f, q, own, tot, s1b, fb,
    wkv, xn, res, ro, gn, oe, ke, ko, sqs, sqr,
    pk, ks1, kf, kq, kown, ktot, ks1b, kfb,
    in_sem, w_sem, out_sem,
    a_send, a_recv, k_send, k_recv, r_send, r_recv,
    p_send, s1_recv, f_recv, q_send, s1b_recv, fb_recv,
    z_send, z_recv, sib_send, sib_recv,
    sq_send, sq_recv, pk_send, ks1_recv, kf_recv, kq_send, ks1b_recv, kfb_recv,
):
    me = lax.axis_index("tensor")
    dp = lax.axis_index("dp")
    y, x = me // 4, lax.rem(me, 4)
    z, core = dp // 2, lax.rem(dp, 2)
    nz = lax.axis_size("dp") // 2
    share = core * PLANES + lax.rem(z, PLANES)

    def at_yx(dy, dx):
        return lax.rem(y + dy, 4) * 4 + lax.rem(x + dx, 4)

    along = (
        ({"tensor": at_yx(0, 1)}, {"tensor": at_yx(0, 3)}),
        ({"tensor": at_yx(1, 0)}, {"tensor": at_yx(3, 0)}),
    )

    def at_z(k):
        return {"dp": lax.rem(z + k + nz, nz) * 2 + core}

    sibling = {"dp": z * 2 + 1 - core}

    def send(src, dst, send_sem, recv_sem, to):
        pltpu.make_async_remote_copy(
            src_ref=src, dst_ref=dst, send_sem=send_sem, recv_sem=recv_sem,
            device_id=to, device_id_type=MESH,
        ).start()

    def wait(ref, sem):
        pltpu.make_async_copy(ref, ref, sem).wait()

    def to_peers(fn):
        for dy, dx in PEERS:
            fn(at_yx(dy, dx))

    barrier = pltpu.get_barrier_semaphore()

    def greet(j):
        pl.semaphore_signal(barrier, inc=1, device_id={"tensor": j}, device_id_type=MESH)

    to_peers(greet)
    for to in (at_z(1), at_z(-1), at_z(2), at_z(-2), sibling):
        pl.semaphore_signal(barrier, inc=1, device_id=to, device_id_type=MESH)

    mine = pl.ds(pl.multiple_of(me * 16, 16), 16)
    my_rows = pl.ds(pl.multiple_of(share * CK, CK), CK)
    my_cols = pl.ds(pl.multiple_of(me * KVB, KVB), KVB)
    loads = [
        pltpu.make_async_copy(attn.at[mine, :], att.at[me], in_sem.at[0]),
        pltpu.make_async_copy(signs, sgn, in_sem.at[1]),
        pltpu.make_async_copy(
            w_kv.at[pl.ds(pl.multiple_of(me * BLK + share * CK, CK), CK), :],
            wkv.at[my_rows, my_cols], in_sem.at[2],
        ),
        pltpu.make_async_copy(out_exp, oe, in_sem.at[3]),
        pltpu.make_async_copy(residual, res, in_sem.at[4]),
        pltpu.make_async_copy(gain, gn, in_sem.at[5]),
        pltpu.make_async_copy(kv_exp, ke, in_sem.at[6]),
    ]
    for copy in loads:
        copy.start()

    w_loads = {}
    for i, (dy, dx) in enumerate(ORDER):
        columns = pl.ds(pl.multiple_of(at_yx(dy, dx) * BLK, BLK), BLK)
        w_loads[dy, dx] = pltpu.make_async_copy(w_out.at[:, columns], w.at[dy, dx], w_sem.at[i])

    pl.semaphore_wait(barrier, N - 1 + 5)

    def send_tokens(j):
        rows = pl.ds(pl.multiple_of(j * 16, 16), 16)
        send(attn.at[rows, :], att.at[me], a_send, a_recv, {"tensor": j})

    to_peers(send_tokens)

    def send_kv_rows(j):
        rows = pl.ds(pl.multiple_of(j * BLK + share * CK, CK), CK)
        send(w_kv.at[rows, :], wkv.at[my_rows, my_cols], k_send, k_recv, {"tensor": j})

    to_peers(send_kv_rows)
    for dy, dx in ORDER:
        w_loads[dy, dx].start()

    loads[0].wait()
    loads[1].wait()
    wait(att.at[pl.ds(0, N - 1)], a_recv)
    for s in range(N):
        heads = []
        for h in range(LH):
            sign = (2 * sgn[s * LH + h] - 1).astype(F32)
            heads.append(att[s, :, h * HD : (h + 1) * HD].astype(F32) * sign)
        for h, val in enumerate(hadamard(heads)):
            mixed[s, :, h * HD : (h + 1) * HD] = val
    for h in range(LH):
        at = slice(h * HD, (h + 1) * HD)
        for g, val in enumerate(hadamard([mixed[s, :, at] for s in range(N)])):
            turned[g, :, at] = (val * 0.125).astype(BF16)

    def send_turned(j):
        send(turned.at[j], rot.at[mine, :], r_send, r_recv, {"tensor": j})

    to_peers(send_turned)
    rot[mine, :] = turned[me]

    def z_start():
        loads[2].wait()
        wait(wkv.at[pl.ds(0, CK), pl.ds(0, (N - 1) * KVB)], k_recv)
        part = wkv.at[my_rows, :]
        for k in (1, -1):
            send(part, part, z_send, z_recv, at_z(k))
        for i, k in enumerate((2, -2)):
            rows = pl.ds(pl.multiple_of(share * CK + i * (CK // 2), CK // 2), CK // 2)
            send(wkv.at[rows, :], wkv.at[rows, :], z_send, z_recv, at_z(k))

    def z_finish():
        wait(wkv.at[pl.ds(0, (PLANES - 1) * CK), :], z_recv)
        rows = pl.ds(pl.multiple_of(core * (BLK // 2), BLK // 2), BLK // 2)
        send(wkv.at[rows, :], wkv.at[rows, :], sib_send, sib_recv, sibling)

    def block(half, c, a):
        return (c, a) if half == 0 else (a, c)

    def rows_of(half):
        return pl.ds(half * HALF, HALF)

    def matmul(dy, dx):
        w_loads[dy, dx].wait()
        pb[dy, dx] = jnp.dot(rot[...], w[dy, dx], preferred_element_type=F32).astype(BF16)

    def first_far(half, c):
        dy, dx = block(half, c, 2)
        for way in range(2):
            send(
                pb.at[dy, dx, pl.ds(half * HALF, HALF), pl.ds(way * HCOL, HCOL)],
                s1.at[half, c, way], p_send, s1_recv.at[half, c, way], along[half][way],
            )

    def first_near(half, c):
        rows = rows_of(half)
        for way, a in enumerate((1, 3)):
            dy, dx = block(half, c, a)
            part = pl.ds(way * HCOL, HCOL)
            wait(s1.at[half, c, way], s1_recv.at[half, c, way])
            pb[dy, dx, rows, part] = (
                pb[dy, dx, rows, part].astype(F32) + s1[half, c, way].astype(F32)
            ).astype(BF16)
            send(
                pb.at[dy, dx, rows, :], f.at[half, c, way],
                p_send, f_recv.at[half, c, way], along[half][way],
            )

    def second(half, c):
        dy, dx = block(half, c, 0)
        total = pb[dy, dx, rows_of(half), :].astype(F32)
        for way in range(2):
            wait(f.at[half, c, way], f_recv.at[half, c, way])
            total = total + f[half, c, way].astype(F32)
        if c == 0:
            own[half] = total
            return
        if c == 2:
            q[half, 1] = total.astype(BF16)
            for way in range(2):
                send(
                    q.at[half, 1, :, pl.ds(way * HCOL, HCOL)], s1b.at[half, way],
                    q_send, s1b_recv.at[half, way], along[1 - half][way],
                )
            return
        way = 0 if c == 1 else 1
        rest = slice((1 - way) * HCOL, (2 - way) * HCOL)
        tot[half, way] = total[:, way * HCOL : (way + 1) * HCOL]
        q[half, c - 1, :, rest] = total[:, rest].astype(BF16)

    def second_near(half):
        for way, c in enumerate((1, 3)):
            wait(s1b.at[half, way], s1b_recv.at[half, way])
            q[half, c - 1, :, way * HCOL : (way + 1) * HCOL] = (
                tot[half, way] + s1b[half, way].astype(F32)
            ).astype(BF16)
            send(
                q.at[half, c - 1], fb.at[half, way],
                q_send, fb_recv.at[half, way], along[1 - half][way],
            )

    def residual_rows(half):
        rows = rows_of(half)
        total = own[half]
        for way in range(2):
            wait(fb.at[half, way], fb_recv.at[half, way])
            total = total + fb[half, way].astype(F32)
        out = (res[rows, :].astype(F32) + total * jnp.exp2(oe[...].astype(F32))).astype(BF16)
        ro[rows, :] = out
        pltpu.make_async_copy(ro.at[rows, :], resid_out.at[rows, :], out_sem.at[half]).start()
        hidden = out.astype(F32)
        xn[rows, :] = (hidden * gn[...].astype(F32).reshape(1, BLK)).astype(BF16)
        column = jnp.sum(hidden * hidden, axis=1, keepdims=True)
        return jnp.transpose(jnp.broadcast_to(column, (HALF, LANES)))[:8, :]

    def send_squares(first_half, second_half):
        index = lax.broadcasted_iota(jnp.int32, (8, LANES), 0)
        sqs[...] = jnp.where(index == 0, first_half, second_half)
        sqr[me] = sqs[...]

        def send_square(j):
            send(sqs, sqr.at[me], sq_send, sq_recv, {"tensor": j})

        to_peers(send_square)

    def product(dy):
        yy = lax.rem(y + dy, 4)
        columns = pl.ds(pl.multiple_of(yy * 4 * KVB, 4 * KVB), 4 * KVB)
        part = jnp.dot(xn[...], wkv[:, columns], preferred_element_type=F32).astype(BF16)
        for k in range(4):
            pk[dy, lax.rem(k + 4 - x, 4)] = part[:, k * KVB : (k + 1) * KVB]

    def kv_first_far(half, c):
        dy, dx = block(half, c, 2)
        for way in range(2):
            send(
                pk.at[dy, dx, pl.ds(half * HALF + way * HROW, HROW), :], ks1.at[half, c, way],
                pk_send, ks1_recv.at[half, c, way], along[half][way],
            )

    def kv_first_near(half, c):
        for way, a in enumerate((1, 3)):
            dy, dx = block(half, c, a)
            part = pl.ds(half * HALF + way * HROW, HROW)
            wait(ks1.at[half, c, way], ks1_recv.at[half, c, way])
            pk[dy, dx, part, :] = (
                pk[dy, dx, part, :].astype(F32) + ks1[half, c, way].astype(F32)
            ).astype(BF16)
            send(
                pk.at[dy, dx, rows_of(half), :], kf.at[half, c, way],
                pk_send, kf_recv.at[half, c, way], along[half][way],
            )

    def kv_second(half, c):
        dy, dx = block(half, c, 0)
        total = pk[dy, dx, rows_of(half), :].astype(F32)
        for way in range(2):
            wait(kf.at[half, c, way], kf_recv.at[half, c, way])
            total = total + kf[half, c, way].astype(F32)
        if c == 0:
            kown[half] = total
            return
        if c == 2:
            kq[half, 1] = total.astype(BF16)
            for way in range(2):
                send(
                    kq.at[half, 1, pl.ds(way * HROW, HROW), :], ks1b.at[half, way],
                    kq_send, ks1b_recv.at[half, way], along[1 - half][way],
                )
            return
        way = 0 if c == 1 else 1
        rest = slice((1 - way) * HROW, (2 - way) * HROW)
        ktot[half, way] = total[way * HROW : (way + 1) * HROW, :]
        kq[half, c - 1, rest, :] = total[rest, :].astype(BF16)

    def kv_second_near(half):
        for way, c in enumerate((1, 3)):
            wait(ks1b.at[half, way], ks1b_recv.at[half, way])
            kq[half, c - 1, way * HROW : (way + 1) * HROW, :] = (
                ktot[half, way] + ks1b[half, way].astype(F32)
            ).astype(BF16)
            send(
                kq.at[half, c - 1], kfb.at[half, way],
                kq_send, kfb_recv.at[half, way], along[1 - half][way],
            )

    def row_scales():
        wait(sqr.at[pl.ds(0, N - 1)], sq_recv)
        total_sq = sqr[0]
        for s in range(1, N):
            total_sq = total_sq + sqr[s]
        inv = lax.rsqrt(total_sq / D + 1e-05)
        return [
            jnp.transpose(jnp.broadcast_to(inv[half : half + 1, :], (LANES, HALF)))
            * jnp.exp2(ke[...].astype(F32))
            for half in range(2)
        ]

    def finish(half, scale):
        total = kown[half]
        for way in range(2):
            wait(kfb.at[half, way], kfb_recv.at[half, way])
            total = total + kfb[half, way].astype(F32)
        rows = rows_of(half)
        ko[rows, :] = (total * scale).astype(BF16)
        pltpu.make_async_copy(ko.at[rows, :], kv_out.at[rows, :], out_sem.at[2 + half]).start()

    z_start()
    wait(rot.at[pl.ds(0, (N - 1) * 16), :], r_recv)

    for i, (dy, dx) in enumerate(ORDER):
        matmul(dy, dx)
        if dx == 2:
            first_far(0, dy)
        if dy == 2:
            first_far(1, dx)
        for c in {6: (2,), 10: (1, 3), 14: (0,)}.get(i, ()):
            first_near(0, c)
            first_near(1, c)
    for i in range(3, 7):
        loads[i].wait()
    for c in CHUNKS:
        second(0, c)
        second(1, c)
        if c == 1:
            z_finish()
    second_near(0)
    second_near(1)
    squares = [residual_rows(0), residual_rows(1)]
    send_squares(*squares)
    wait(wkv.at[pl.ds(0, BLK // 2), :], sib_recv)
    for c in CHUNKS:
        product(c)
        kv_first_far(0, c)
        if c == 2:
            for a in CHUNKS:
                kv_first_far(1, a)
    for c in CHUNKS:
        kv_first_near(0, c)
        kv_first_near(1, c)
    scales = row_scales()
    for c in CHUNKS:
        kv_second(0, c)
        kv_second(1, c)
    kv_second_near(0)
    kv_second_near(1)
    finish(0, scales[0])
    finish(1, scales[1])

    wait(att.at[pl.ds(0, N - 1)], a_send)
    wait(wkv.at[pl.ds(0, CK), pl.ds(0, (N - 1) * KVB)], k_send)
    wait(turned.at[pl.ds(0, N - 1)], r_send)
    wait(pb.at[pl.ds(0, 3)], p_send)
    wait(pb.at[0, pl.ds(0, 3)], q_send)
    wait(wkv.at[pl.ds(0, (PLANES - 1) * CK), :], z_send)
    wait(wkv.at[pl.ds(0, BLK // 2), :], sib_send)
    wait(sqr.at[pl.ds(0, N - 1)], sq_send)
    wait(pk.at[pl.ds(0, 3)], pk_send)
    wait(pk.at[0, pl.ds(0, 3)], kq_send)
    for half in range(2):
        rows = rows_of(half)
        pltpu.make_async_copy(ro.at[rows, :], resid_out.at[rows, :], out_sem.at[half]).wait()
        pltpu.make_async_copy(ko.at[rows, :], kv_out.at[rows, :], out_sem.at[2 + half]).wait()


def body(attn_out, head_signs, w_out, out_exp, residual, norm_gain, w_kv, kv_exp):
    vmem = pltpu.VMEM
    dma = pltpu.SemaphoreType.DMA
    scratch = [
        pltpu.SMEM((N * LH,), jnp.int32),
        vmem((N, 16, BLK), BF16),
        vmem((N, 16, BLK), F32),
        vmem((N, 16, BLK), BF16),
        vmem((TOK, BLK), BF16),
        vmem((4, 4, BLK, BLK), BF16),
        vmem((4, 4, TOK, BLK), BF16),
        vmem((2, 4, 2, HALF, HCOL), BF16),
        vmem((2, 4, 2, HALF, BLK), BF16),
        vmem((2, 3, HALF, BLK), BF16),
        vmem((2, HALF, BLK), F32),
        vmem((2, 2, HALF, HCOL), F32),
        vmem((2, 2, HALF, HCOL), BF16),
        vmem((2, 2, HALF, BLK), BF16),
        vmem((BLK, N * KVB), BF16),
        vmem((TOK, BLK), BF16),
        vmem((TOK, BLK), BF16),
        vmem((TOK, BLK), BF16),
        vmem((BLK,), BF16),
        vmem((1, BLK), jnp.int32),
        vmem((1, KVB), jnp.int32),
        vmem((TOK, KVB), BF16),
        vmem((8, LANES), F32),
        vmem((N, 8, LANES), F32),
        vmem((4, 4, TOK, KVB), BF16),
        vmem((2, 4, 2, HROW, KVB), BF16),
        vmem((2, 4, 2, HALF, KVB), BF16),
        vmem((2, 3, HALF, KVB), BF16),
        vmem((2, HALF, KVB), F32),
        vmem((2, 2, HROW, KVB), F32),
        vmem((2, 2, HROW, KVB), BF16),
        vmem((2, 2, HALF, KVB), BF16),
        dma((7,)),
        dma((16,)),
        dma((4,)),
        dma, dma, dma, dma, dma, dma,
        dma,
        dma((2, 4, 2)),
        dma((2, 4, 2)),
        dma,
        dma((2, 2)),
        dma((2, 2)),
        dma, dma, dma, dma,
        dma, dma,
        dma,
        dma((2, 4, 2)),
        dma((2, 4, 2)),
        dma,
        dma((2, 2)),
        dma((2, 2)),
    ]
    anywhere = pl.BlockSpec(memory_space=pl.ANY)
    return pl.pallas_call(
        kernel,
        out_shape=(
            jax.ShapeDtypeStruct((TOK, BLK), BF16),
            jax.ShapeDtypeStruct((TOK, KVB), BF16),
        ),
        in_specs=[anywhere] * 8,
        out_specs=(anywhere, anywhere),
        scratch_shapes=scratch,
        compiler_params=pltpu.CompilerParams(
            collective_id=0, has_side_effects=True, vmem_limit_bytes=62 * 1024 * 1024
        ),
    )(
        attn_out, head_signs, w_out, out_exp.reshape(1, BLK), residual,
        norm_gain, w_kv, kv_exp.reshape(1, KVB),
    )


def solution(mesh):
    placed = (
        P("dp", "tensor"),
        P(),
        P("tensor", None),
        P("tensor"),
        P("dp", "tensor"),
        P("tensor"),
        P(None, "tensor"),
        P("tensor"),
    )
    return jax.shard_map(
        body,
        mesh=mesh,
        in_specs=placed,
        out_specs=(P("dp", "tensor"), P("dp", "tensor")),
        check_vma=False,
    )
```

```python
import jax
import jax.numpy as jnp
from jax import lax
from jax.experimental import pallas as pl
from jax.experimental.pallas import tpu as pltpu
from jax.sharding import PartitionSpec as P

MESH = pl.DeviceIdType.MESH
BF16 = jnp.bfloat16
F32 = jnp.float32
HD = 128
LH = 4
N = 16
TOK = 256
BLK = 512
D = N * BLK
KVB = 128
HALF = TOK // 2
HCOL = BLK // 2
LANES = 128
PLANES = 4
SHARES = 2 * PLANES
CK = BLK // SHARES
PEERS = (
    (2, 2), (2, 1), (1, 2), (2, 3), (3, 2), (2, 0), (0, 2), (1, 1),
    (3, 3), (1, 3), (3, 1), (0, 1), (1, 0), (0, 3), (3, 0),
)
CHUNKS = (2, 1, 3, 0)
ORDER = (
    (2, 2), (1, 2), (2, 1), (3, 2), (2, 3), (0, 2), (2, 0), (1, 1),
    (1, 3), (3, 1), (3, 3), (0, 1), (0, 3), (1, 0), (3, 0), (0, 0),
)


def hadamard(vals):
    step = 1
    while step < len(vals):
        out = list(vals)
        for i in range(len(vals)):
            if not i & step:
                out[i] = vals[i] + vals[i | step]
                out[i | step] = vals[i] - vals[i | step]
        vals = out
        step *= 2
    return vals


def kernel(
    attn, signs, w_out, out_exp, residual, gain, w_kv, kv_exp,
    resid_out, kv_out,
    sgn, att, mixed, turned, rot, w, pb, s1, f, q, own, s1b, fb,
    wkv, xn, res, ro, gn, oe, ke, ko, sqs, sqr,
    pk, kf, kq, kown, kfb,
    in_sem, w_sem, out_sem,
    a_send, a_recv, k_send, k_recv, r_send, r_recv,
    p_send, s1_recv, f_recv, q_send, s1b_recv, fb_recv,
    z_send, z_recv, sib_send, sib_recv,
    sq_send, sq_recv, pk_send, kf_recv, kq_send, kfb_recv,
):
    me = lax.axis_index("tensor")
    dp = lax.axis_index("dp")
    y, x = me // 4, lax.rem(me, 4)
    z, core = dp // 2, lax.rem(dp, 2)
    nz = lax.axis_size("dp") // 2
    share = core * PLANES + lax.rem(z, PLANES)

    def at_yx(dy, dx):
        return lax.rem(y + dy, 4) * 4 + lax.rem(x + dx, 4)

    along = (
        ({"tensor": at_yx(0, 1)}, {"tensor": at_yx(0, 3)}),
        ({"tensor": at_yx(1, 0)}, {"tensor": at_yx(3, 0)}),
    )

    def at_z(k):
        return {"dp": lax.rem(z + k + nz, nz) * 2 + core}

    top = nz - 1
    z_peers = (
        (z < top, 1), (z > 0, -1), (z < top - 1, 2), (z > 1, -2),
        ((z == 0) | (z == top - 3), 3), ((z == 3) | (z == top), -3),
    )
    z_sends = (
        (z < top, 1, 0, CK), (z > 0, -1, 0, CK),
        (z < top - 1, 2, 0, CK // 2), ((z < top - 1) & (z >= top - 3), 2, CK // 2, CK // 2),
        (z > 1, -2, CK // 2, CK // 2), ((z > 1) & (z <= 3), -2, 0, CK // 2),
        (z == top - 3, 3, 0, CK), (z == 3, -3, 0, CK),
    )

    sibling = {"dp": z * 2 + 1 - core}

    def send(src, dst, send_sem, recv_sem, to):
        pltpu.make_async_remote_copy(
            src_ref=src, dst_ref=dst, send_sem=send_sem, recv_sem=recv_sem,
            device_id=to, device_id_type=MESH,
        ).start()

    def wait(ref, sem):
        pltpu.make_async_copy(ref, ref, sem).wait()

    def to_peers(fn):
        for dy, dx in PEERS:
            fn(at_yx(dy, dx))

    barrier = pltpu.get_barrier_semaphore()

    def greet(j):
        pl.semaphore_signal(barrier, inc=1, device_id={"tensor": j}, device_id_type=MESH)

    to_peers(greet)
    pl.semaphore_signal(barrier, inc=1, device_id=sibling, device_id_type=MESH)
    for there, k in z_peers:

        @pl.when(there)
        def _(k=k):
            pl.semaphore_signal(barrier, inc=1, device_id=at_z(k), device_id_type=MESH)


    mine = pl.ds(pl.multiple_of(me * 16, 16), 16)
    my_rows = pl.ds(pl.multiple_of(share * CK, CK), CK)
    my_cols = pl.ds(pl.multiple_of(me * KVB, KVB), KVB)
    loads = [
        pltpu.make_async_copy(attn.at[mine, :], att.at[me], in_sem.at[0]),
        pltpu.make_async_copy(signs, sgn, in_sem.at[1]),
        pltpu.make_async_copy(
            w_kv.at[pl.ds(pl.multiple_of(me * BLK + share * CK, CK), CK), :],
            wkv.at[my_rows, my_cols], in_sem.at[2],
        ),
        pltpu.make_async_copy(out_exp, oe, in_sem.at[3]),
        pltpu.make_async_copy(residual, res, in_sem.at[4]),
        pltpu.make_async_copy(gain, gn, in_sem.at[5]),
        pltpu.make_async_copy(kv_exp, ke, in_sem.at[6]),
    ]
    for copy in loads:
        copy.start()

    w_loads = {}
    for i, (dy, dx) in enumerate(ORDER):
        columns = pl.ds(pl.multiple_of(at_yx(dy, dx) * BLK, BLK), BLK)
        w_loads[dy, dx] = pltpu.make_async_copy(w_out.at[:, columns], w.at[dy, dx], w_sem.at[i])

    pl.semaphore_wait(barrier, N + sum(there.astype(jnp.int32) for there, _ in z_peers))

    def send_tokens(j):
        rows = pl.ds(pl.multiple_of(j * 16, 16), 16)
        send(attn.at[rows, :], att.at[me], a_send, a_recv, {"tensor": j})

    to_peers(send_tokens)

    def send_kv_rows(j):
        rows = pl.ds(pl.multiple_of(j * BLK + share * CK, CK), CK)
        send(w_kv.at[rows, :], wkv.at[my_rows, my_cols], k_send, k_recv, {"tensor": j})

    to_peers(send_kv_rows)
    for dy, dx in ORDER:
        w_loads[dy, dx].start()

    loads[0].wait()
    loads[1].wait()
    wait(att.at[pl.ds(0, N - 1)], a_recv)
    for s in range(N):
        heads = []
        for h in range(LH):
            sign = (2 * sgn[s * LH + h] - 1).astype(F32)
            heads.append(att[s, :, h * HD : (h + 1) * HD].astype(F32) * sign)
        for h, val in enumerate(hadamard(heads)):
            mixed[s, :, h * HD : (h + 1) * HD] = val
    for h in range(LH):
        at = slice(h * HD, (h + 1) * HD)
        for g, val in enumerate(hadamard([mixed[s, :, at] for s in range(N)])):
            turned[g, :, at] = (val * 0.125).astype(BF16)

    def send_turned(j):
        send(turned.at[j], rot.at[mine, :], r_send, r_recv, {"tensor": j})

    to_peers(send_turned)
    rot[mine, :] = turned[me]

    def z_start():
        loads[2].wait()
        wait(wkv.at[pl.ds(0, CK), pl.ds(0, (N - 1) * KVB)], k_recv)
        for there, k, low, count in z_sends:

            @pl.when(there)
            def _(k=k, low=low, count=count):
                rows = pl.ds(pl.multiple_of(share * CK + low, CK // 2), count)
                send(wkv.at[rows, :], wkv.at[rows, :], z_send, z_recv, at_z(k))

    def z_finish():
        wait(wkv.at[pl.ds(0, (PLANES - 1) * CK), :], z_recv)
        rows = pl.ds(pl.multiple_of(core * (BLK // 2), BLK // 2), BLK // 2)
        send(wkv.at[rows, :], wkv.at[rows, :], sib_send, sib_recv, sibling)

    def block(half, c, a):
        return (c, a) if half == 0 else (a, c)

    def rows_of(half):
        return pl.ds(half * HALF, HALF)

    def matmul(dy, dx):
        w_loads[dy, dx].wait()
        pb[dy, dx] = jnp.dot(rot[...], w[dy, dx], preferred_element_type=F32).astype(BF16)

    def first_far(half, c):
        dy, dx = block(half, c, 2)
        for way in range(2):
            send(
                pb.at[dy, dx, pl.ds(half * HALF, HALF), pl.ds(way * HCOL, HCOL)],
                s1.at[half, c, way], p_send, s1_recv.at[half, c, way], along[half][way],
            )

    def first_near(half, c):
        rows = rows_of(half)
        for way, a in enumerate((1, 3)):
            dy, dx = block(half, c, a)
            part = pl.ds(way * HCOL, HCOL)
            wait(s1.at[half, c, way], s1_recv.at[half, c, way])
            pb[dy, dx, rows, part] = (
                pb[dy, dx, rows, part].astype(F32) + s1[half, c, way].astype(F32)
            ).astype(BF16)
            send(
                pb.at[dy, dx, rows, :], f.at[half, c, way],
                p_send, f_recv.at[half, c, way], along[half][way],
            )

    def second(half, c):
        dy, dx = block(half, c, 0)
        total = pb[dy, dx, rows_of(half), :].astype(F32)
        for way in range(2):
            wait(f.at[half, c, way], f_recv.at[half, c, way])
            total = total + f[half, c, way].astype(F32)
        if c == 0:
            own[half] = total
            return
        if c == 2:
            q[half, 1] = total.astype(BF16)
            for way in range(2):
                send(
                    q.at[half, 1, :, pl.ds(way * HCOL, HCOL)], s1b.at[half, way],
                    q_send, s1b_recv.at[half, way], along[1 - half][way],
                )
            return
        way = 0 if c == 1 else 1
        part = slice(way * HCOL, (way + 1) * HCOL)
        rest = slice((1 - way) * HCOL, (2 - way) * HCOL)
        q[half, c - 1, :, rest] = total[:, rest].astype(BF16)
        wait(s1b.at[half, way], s1b_recv.at[half, way])
        q[half, c - 1, :, part] = (total[:, part] + s1b[half, way].astype(F32)).astype(BF16)
        send(
            q.at[half, c - 1], fb.at[half, way],
            q_send, fb_recv.at[half, way], along[1 - half][way],
        )

    def residual_rows(half):
        rows = rows_of(half)
        total = own[half]
        for way in range(2):
            wait(fb.at[half, way], fb_recv.at[half, way])
            total = total + fb[half, way].astype(F32)
        out = (res[rows, :].astype(F32) + total * jnp.exp2(oe[...].astype(F32))).astype(BF16)
        ro[rows, :] = out
        pltpu.make_async_copy(ro.at[rows, :], resid_out.at[rows, :], out_sem.at[half]).start()
        hidden = out.astype(F32)
        xn[rows, :] = (hidden * gn[...].astype(F32).reshape(1, BLK)).astype(BF16)
        column = jnp.sum(hidden * hidden, axis=1, keepdims=True)
        return jnp.transpose(jnp.broadcast_to(column, (HALF, LANES)))[:8, :]

    def send_squares(first_half, second_half):
        index = lax.broadcasted_iota(jnp.int32, (8, LANES), 0)
        sqs[...] = jnp.where(index == 0, first_half, second_half)
        sqr[me] = sqs[...]

        def send_square(j):
            send(sqs, sqr.at[me], sq_send, sq_recv, {"tensor": j})

        to_peers(send_square)

    def product(dy):
        yy = lax.rem(y + dy, 4)
        columns = pl.ds(pl.multiple_of(yy * 4 * KVB, 4 * KVB), 4 * KVB)
        part = jnp.dot(xn[...], wkv[:, columns], preferred_element_type=F32).astype(BF16)
        for k in range(4):
            pk[dy, lax.rem(k + 4 - x, 4)] = part[:, k * KVB : (k + 1) * KVB]

    def kv_first(half, c):
        for a in (2, 1, 3):
            dy, dx = block(half, c, a)
            to = at_yx(0, a) if half == 0 else at_yx(a, 0)
            send(
                pk.at[dy, dx, rows_of(half), :], kf.at[half, c, a - 1],
                pk_send, kf_recv.at[half, c, a - 1], {"tensor": to},
            )

    def kv_second(half, c):
        dy, dx = block(half, c, 0)
        total = pk[dy, dx, rows_of(half), :].astype(F32)
        for k in range(3):
            wait(kf.at[half, c, k], kf_recv.at[half, c, k])
            total = total + kf[half, c, k].astype(F32)
        if c == 0:
            kown[half] = total
            return
        kq[half, c - 1] = total.astype(BF16)
        to = at_yx(c, 0) if half == 0 else at_yx(0, c)
        send(
            kq.at[half, c - 1], kfb.at[half, c - 1],
            kq_send, kfb_recv.at[half, c - 1], {"tensor": to},
        )

    def row_scales():
        wait(sqr.at[pl.ds(0, N - 1)], sq_recv)
        total_sq = sqr[0]
        for s in range(1, N):
            total_sq = total_sq + sqr[s]
        inv = lax.rsqrt(total_sq / D + 1e-05)
        return [
            jnp.transpose(jnp.broadcast_to(inv[half : half + 1, :], (LANES, HALF)))
            * jnp.exp2(ke[...].astype(F32))
            for half in range(2)
        ]

    def finish(half, scale):
        total = kown[half]
        for k in range(3):
            wait(kfb.at[half, k], kfb_recv.at[half, k])
            total = total + kfb[half, k].astype(F32)
        rows = rows_of(half)
        ko[rows, :] = (total * scale).astype(BF16)
        pltpu.make_async_copy(ko.at[rows, :], kv_out.at[rows, :], out_sem.at[2 + half]).start()

    z_start()
    wait(rot.at[pl.ds(0, (N - 1) * 16), :], r_recv)

    for i, (dy, dx) in enumerate(ORDER):
        matmul(dy, dx)
        if dx == 2:
            first_far(0, dy)
        if dy == 2:
            first_far(1, dx)
        for c in {6: (2,), 10: (1, 3), 14: (0,)}.get(i, ()):
            first_near(0, c)
            first_near(1, c)
    for i in range(3, 7):
        loads[i].wait()
    for c in CHUNKS:
        second(0, c)
        second(1, c)
        if c == 1:
            z_finish()
    squares = [residual_rows(0), residual_rows(1)]
    send_squares(*squares)
    wait(wkv.at[pl.ds(0, BLK // 2), :], sib_recv)
    for c in CHUNKS:
        product(c)
        kv_first(0, c)
        if c == 3:
            for k in CHUNKS:
                kv_first(1, k)
    for c in CHUNKS:
        if c == 0:
            scales = row_scales()
        kv_second(0, c)
        kv_second(1, c)
    finish(0, scales[0])
    finish(1, scales[1])

    wait(att.at[pl.ds(0, N - 1)], a_send)
    wait(wkv.at[pl.ds(0, CK), pl.ds(0, (N - 1) * KVB)], k_send)
    wait(turned.at[pl.ds(0, N - 1)], r_send)
    wait(pb.at[pl.ds(0, 3)], p_send)
    wait(pb.at[0, pl.ds(0, 3)], q_send)
    for there, _, _, count in z_sends:

        @pl.when(there)
        def _(count=count):
            wait(wkv.at[pl.ds(0, count), :], z_send)

    wait(wkv.at[pl.ds(0, BLK // 2), :], sib_send)
    wait(sqr.at[pl.ds(0, N - 1)], sq_send)
    wait(pk.at[pl.ds(0, 3)], pk_send)
    wait(pk.at[0, pl.ds(0, 3)], kq_send)
    for half in range(2):
        rows = rows_of(half)
        pltpu.make_async_copy(ro.at[rows, :], resid_out.at[rows, :], out_sem.at[half]).wait()
        pltpu.make_async_copy(ko.at[rows, :], kv_out.at[rows, :], out_sem.at[2 + half]).wait()


def body(attn_out, head_signs, w_out, out_exp, residual, norm_gain, w_kv, kv_exp):
    vmem = pltpu.VMEM
    dma = pltpu.SemaphoreType.DMA
    scratch = [
        pltpu.SMEM((N * LH,), jnp.int32),
        vmem((N, 16, BLK), BF16),
        vmem((N, 16, BLK), F32),
        vmem((N, 16, BLK), BF16),
        vmem((TOK, BLK), BF16),
        vmem((4, 4, BLK, BLK), BF16),
        vmem((4, 4, TOK, BLK), BF16),
        vmem((2, 4, 2, HALF, HCOL), BF16),
        vmem((2, 4, 2, HALF, BLK), BF16),
        vmem((2, 3, HALF, BLK), BF16),
        vmem((2, HALF, BLK), F32),
        vmem((2, 2, HALF, HCOL), BF16),
        vmem((2, 2, HALF, BLK), BF16),
        vmem((BLK, N * KVB), BF16),
        vmem((TOK, BLK), BF16),
        vmem((TOK, BLK), BF16),
        vmem((TOK, BLK), BF16),
        vmem((BLK,), BF16),
        vmem((1, BLK), jnp.int32),
        vmem((1, KVB), jnp.int32),
        vmem((TOK, KVB), BF16),
        vmem((8, LANES), F32),
        vmem((N, 8, LANES), F32),
        vmem((4, 4, TOK, KVB), BF16),
        vmem((2, 4, 3, HALF, KVB), BF16),
        vmem((2, 3, HALF, KVB), BF16),
        vmem((2, HALF, KVB), F32),
        vmem((2, 3, HALF, KVB), BF16),
        dma((7,)),
        dma((16,)),
        dma((4,)),
        dma, dma, dma, dma, dma, dma,
        dma,
        dma((2, 4, 2)),
        dma((2, 4, 2)),
        dma,
        dma((2, 2)),
        dma((2, 2)),
        dma, dma, dma, dma,
        dma, dma,
        dma,
        dma((2, 4, 3)),
        dma,
        dma((2, 3)),
    ]
    anywhere = pl.BlockSpec(memory_space=pl.ANY)
    return pl.pallas_call(
        kernel,
        out_shape=(
            jax.ShapeDtypeStruct((TOK, BLK), BF16),
            jax.ShapeDtypeStruct((TOK, KVB), BF16),
        ),
        in_specs=[anywhere] * 8,
        out_specs=(anywhere, anywhere),
        scratch_shapes=scratch,
        compiler_params=pltpu.CompilerParams(
            collective_id=0, has_side_effects=True, vmem_limit_bytes=62 * 1024 * 1024
        ),
    )(
        attn_out, head_signs, w_out, out_exp.reshape(1, BLK), residual,
        norm_gain, w_kv, kv_exp.reshape(1, KVB),
    )


def solution(mesh):
    placed = (
        P("dp", "tensor"),
        P(),
        P("tensor", None),
        P("tensor"),
        P("dp", "tensor"),
        P("tensor"),
        P(None, "tensor"),
        P("tensor"),
    )
    return jax.shard_map(
        body,
        mesh=mesh,
        in_specs=placed,
        out_specs=(P("dp", "tensor"), P("dp", "tensor")),
        check_vma=False,
    )
```

```python
import jax
import jax.numpy as jnp
from jax import lax
from jax.experimental import pallas as pl
from jax.experimental.pallas import tpu as pltpu
from jax.sharding import PartitionSpec as P

MESH = pl.DeviceIdType.MESH
BF16 = jnp.bfloat16
F32 = jnp.float32
HD = 128
LH = 4
N = 16
TOK = 256
BLK = 512
D = N * BLK
KVB = 128
HALF = TOK // 2
HCOL = BLK // 2
LANES = 128
PLANES = 2
SHARES = 2 * PLANES
CK = BLK // SHARES
PEERS = (
    (2, 2), (2, 1), (1, 2), (2, 3), (3, 2), (2, 0), (0, 2), (1, 1),
    (3, 3), (1, 3), (3, 1), (0, 1), (1, 0), (0, 3), (3, 0),
)
CHUNKS = (2, 1, 3, 0)
ORDER = (
    (2, 2), (1, 2), (2, 1), (3, 2), (2, 3), (0, 2), (2, 0), (1, 1),
    (1, 3), (3, 1), (3, 3), (0, 1), (0, 3), (1, 0), (3, 0), (0, 0),
)


def hadamard(vals):
    step = 1
    while step < len(vals):
        out = list(vals)
        for i in range(len(vals)):
            if not i & step:
                out[i] = vals[i] + vals[i | step]
                out[i | step] = vals[i] - vals[i | step]
        vals = out
        step *= 2
    return vals


def kernel(
    attn, signs, w_out, out_exp, residual, gain, w_kv, kv_exp,
    resid_out, kv_out,
    sgn, att, mixed, turned, rot, w, pb, s1, f, q, own, s1b, fb,
    wkv, xn, res, ro, gn, oe, ke, ko, sqs, sqr,
    pk, kf, kq, kown, kfb,
    in_sem, w_sem, out_sem,
    a_send, a_recv, k_send, k_recv, r_send, r_recv,
    p_send, s1_recv, f_recv, q_send, s1b_recv, fb_recv,
    z_send, z_recv, sib_send, sib_recv,
    sq_send, sq_recv, pk_send, kf_recv, kq_send, kfb_recv,
):
    me = lax.axis_index("tensor")
    dp = lax.axis_index("dp")
    y, x = me // 4, lax.rem(me, 4)
    z, core = dp // 2, lax.rem(dp, 2)
    nz = lax.axis_size("dp") // 2
    share = core * PLANES + lax.rem(z, PLANES)

    def at_yx(dy, dx):
        return lax.rem(y + dy, 4) * 4 + lax.rem(x + dx, 4)

    along = (
        ({"tensor": at_yx(0, 1)}, {"tensor": at_yx(0, 3)}),
        ({"tensor": at_yx(1, 0)}, {"tensor": at_yx(3, 0)}),
    )

    def at_z(k):
        return {"dp": lax.rem(z + k + nz, nz) * 2 + core}

    top = nz - 1
    z_peers = ((z < top, 1), (z > 0, -1))
    z_sends = (
        (z < top, 1, 0, CK // 2), (z > 0, -1, CK // 2, CK // 2),
        (z == top - 1, 1, CK // 2, CK // 2), (z == 1, -1, 0, CK // 2),
    )
    sibling = {"dp": z * 2 + 1 - core}

    def send(src, dst, send_sem, recv_sem, to):
        pltpu.make_async_remote_copy(
            src_ref=src, dst_ref=dst, send_sem=send_sem, recv_sem=recv_sem,
            device_id=to, device_id_type=MESH,
        ).start()

    def wait(ref, sem):
        pltpu.make_async_copy(ref, ref, sem).wait()

    def to_peers(fn):
        for dy, dx in PEERS:
            fn(at_yx(dy, dx))

    barrier = pltpu.get_barrier_semaphore()

    def greet(j):
        pl.semaphore_signal(barrier, inc=1, device_id={"tensor": j}, device_id_type=MESH)

    to_peers(greet)
    pl.semaphore_signal(barrier, inc=1, device_id=sibling, device_id_type=MESH)
    for there, k in z_peers:

        @pl.when(there)
        def _(k=k):
            pl.semaphore_signal(barrier, inc=1, device_id=at_z(k), device_id_type=MESH)


    mine = pl.ds(pl.multiple_of(me * 16, 16), 16)
    my_rows = pl.ds(pl.multiple_of(share * CK, CK), CK)
    my_cols = pl.ds(pl.multiple_of(me * KVB, KVB), KVB)
    loads = [
        pltpu.make_async_copy(attn.at[mine, :], att.at[me], in_sem.at[0]),
        pltpu.make_async_copy(signs, sgn, in_sem.at[1]),
        pltpu.make_async_copy(
            w_kv.at[pl.ds(pl.multiple_of(me * BLK + share * CK, CK), CK), :],
            wkv.at[my_rows, my_cols], in_sem.at[2],
        ),
        pltpu.make_async_copy(out_exp, oe, in_sem.at[3]),
        pltpu.make_async_copy(residual, res, in_sem.at[4]),
        pltpu.make_async_copy(gain, gn, in_sem.at[5]),
        pltpu.make_async_copy(kv_exp, ke, in_sem.at[6]),
    ]
    for copy in loads:
        copy.start()

    w_loads = {}
    for i, (dy, dx) in enumerate(ORDER):
        columns = pl.ds(pl.multiple_of(at_yx(dy, dx) * BLK, BLK), BLK)
        w_loads[dy, dx] = pltpu.make_async_copy(w_out.at[:, columns], w.at[dy, dx], w_sem.at[i])

    for dy, dx in ORDER:
        w_loads[dy, dx].start()
    pl.semaphore_wait(barrier, N + sum(there.astype(jnp.int32) for there, _ in z_peers))

    def send_tokens(j):
        rows = pl.ds(pl.multiple_of(j * 16, 16), 16)
        send(attn.at[rows, :], att.at[me], a_send, a_recv, {"tensor": j})

    to_peers(send_tokens)

    def send_kv_rows(j, part):
        low = part * (CK // 2)
        rows = pl.ds(pl.multiple_of(j * BLK + share * CK + low, CK // 2), CK // 2)
        slot = pl.ds(pl.multiple_of(share * CK + low, CK // 2), CK // 2)
        send(w_kv.at[rows, :], wkv.at[slot, my_cols], k_send, k_recv, {"tensor": j})

    to_peers(lambda j: send_kv_rows(j, 0))

    loads[0].wait()
    loads[1].wait()
    wait(att.at[pl.ds(0, N - 1)], a_recv)
    for s in range(N):
        heads = []
        for h in range(LH):
            sign = (2 * sgn[s * LH + h] - 1).astype(F32)
            heads.append(att[s, :, h * HD : (h + 1) * HD].astype(F32) * sign)
        for h, val in enumerate(hadamard(heads)):
            mixed[s, :, h * HD : (h + 1) * HD] = val
    for h in range(LH):
        at = slice(h * HD, (h + 1) * HD)
        for g, val in enumerate(hadamard([mixed[s, :, at] for s in range(N)])):
            turned[g, :, at] = (val * 0.125).astype(BF16)

    def send_turned(j):
        send(turned.at[j], rot.at[mine, :], r_send, r_recv, {"tensor": j})

    to_peers(send_turned)
    to_peers(lambda j: send_kv_rows(j, 1))
    rot[mine, :] = turned[me]

    def z_start():
        loads[2].wait()
        wait(wkv.at[pl.ds(0, CK), pl.ds(0, (N - 1) * KVB)], k_recv)
        for there, k, low, count in z_sends:

            @pl.when(there)
            def _(k=k, low=low, count=count):
                rows = pl.ds(pl.multiple_of(share * CK + low, CK // 2), count)
                send(wkv.at[rows, :], wkv.at[rows, :], z_send, z_recv, at_z(k))

    def z_finish():
        wait(wkv.at[pl.ds(0, (PLANES - 1) * CK), :], z_recv)
        rows = pl.ds(pl.multiple_of(core * (BLK // 2), BLK // 2), BLK // 2)
        send(wkv.at[rows, :], wkv.at[rows, :], sib_send, sib_recv, sibling)

    def block(half, c, a):
        return (c, a) if half == 0 else (a, c)

    def rows_of(half):
        return pl.ds(half * HALF, HALF)

    def matmul(dy, dx):
        w_loads[dy, dx].wait()
        pb[dy, dx] = jnp.dot(rot[...], w[dy, dx], preferred_element_type=F32).astype(BF16)

    def first_far(half, c):
        dy, dx = block(half, c, 2)
        for way in range(2):
            send(
                pb.at[dy, dx, pl.ds(half * HALF, HALF), pl.ds(way * HCOL, HCOL)],
                s1.at[half, c, way], p_send, s1_recv.at[half, c, way], along[half][way],
            )

    def first_near(half, c):
        rows = rows_of(half)
        for way, a in enumerate((1, 3)):
            dy, dx = block(half, c, a)
            part = pl.ds(way * HCOL, HCOL)
            wait(s1.at[half, c, way], s1_recv.at[half, c, way])
            pb[dy, dx, rows, part] = (
                pb[dy, dx, rows, part].astype(F32) + s1[half, c, way].astype(F32)
            ).astype(BF16)
            send(
                pb.at[dy, dx, rows, :], f.at[half, c, way],
                p_send, f_recv.at[half, c, way], along[half][way],
            )

    def second(half, c):
        dy, dx = block(half, c, 0)
        total = pb[dy, dx, rows_of(half), :].astype(F32)
        for way in range(2):
            wait(f.at[half, c, way], f_recv.at[half, c, way])
            total = total + f[half, c, way].astype(F32)
        if c == 0:
            own[half] = total
            return
        if c == 2:
            q[half, 1] = total.astype(BF16)
            for way in range(2):
                send(
                    q.at[half, 1, :, pl.ds(way * HCOL, HCOL)], s1b.at[half, way],
                    q_send, s1b_recv.at[half, way], along[1 - half][way],
                )
            return
        way = 0 if c == 1 else 1
        part = slice(way * HCOL, (way + 1) * HCOL)
        rest = slice((1 - way) * HCOL, (2 - way) * HCOL)
        q[half, c - 1, :, rest] = total[:, rest].astype(BF16)
        wait(s1b.at[half, way], s1b_recv.at[half, way])
        q[half, c - 1, :, part] = (total[:, part] + s1b[half, way].astype(F32)).astype(BF16)
        send(
            q.at[half, c - 1], fb.at[half, way],
            q_send, fb_recv.at[half, way], along[1 - half][way],
        )

    def residual_rows(half):
        rows = rows_of(half)
        total = own[half]
        for way in range(2):
            wait(fb.at[half, way], fb_recv.at[half, way])
            total = total + fb[half, way].astype(F32)
        out = (res[rows, :].astype(F32) + total * jnp.exp2(oe[...].astype(F32))).astype(BF16)
        ro[rows, :] = out
        pltpu.make_async_copy(ro.at[rows, :], resid_out.at[rows, :], out_sem.at[half]).start()
        hidden = out.astype(F32)
        xn[rows, :] = (hidden * gn[...].astype(F32).reshape(1, BLK)).astype(BF16)
        column = jnp.sum(hidden * hidden, axis=1, keepdims=True)
        return jnp.transpose(jnp.broadcast_to(column, (HALF, LANES)))[:8, :]

    def send_squares(first_half, second_half):
        index = lax.broadcasted_iota(jnp.int32, (8, LANES), 0)
        sqs[...] = jnp.where(index == 0, first_half, second_half)
        sqr[me] = sqs[...]

        def send_square(j):
            send(sqs, sqr.at[me], sq_send, sq_recv, {"tensor": j})

        to_peers(send_square)

    def product(dy):
        yy = lax.rem(y + dy, 4)
        columns = pl.ds(pl.multiple_of(yy * 4 * KVB, 4 * KVB), 4 * KVB)
        part = jnp.dot(xn[...], wkv[:, columns], preferred_element_type=F32).astype(BF16)
        for k in range(4):
            pk[dy, lax.rem(k + 4 - x, 4)] = part[:, k * KVB : (k + 1) * KVB]

    def kv_first(half, c):
        for a in (2, 1, 3):
            dy, dx = block(half, c, a)
            to = at_yx(0, a) if half == 0 else at_yx(a, 0)
            send(
                pk.at[dy, dx, rows_of(half), :], kf.at[half, c, a - 1],
                pk_send, kf_recv.at[half, c, a - 1], {"tensor": to},
            )

    def kv_second(half, c):
        dy, dx = block(half, c, 0)
        total = pk[dy, dx, rows_of(half), :].astype(F32)
        for k in range(3):
            wait(kf.at[half, c, k], kf_recv.at[half, c, k])
            total = total + kf[half, c, k].astype(F32)
        if c == 0:
            kown[half] = total
            return
        kq[half, c - 1] = total.astype(BF16)
        to = at_yx(c, 0) if half == 0 else at_yx(0, c)
        send(
            kq.at[half, c - 1], kfb.at[half, c - 1],
            kq_send, kfb_recv.at[half, c - 1], {"tensor": to},
        )

    def row_scales():
        wait(sqr.at[pl.ds(0, N - 1)], sq_recv)
        total_sq = sqr[0]
        for s in range(1, N):
            total_sq = total_sq + sqr[s]
        inv = lax.rsqrt(total_sq / D + 1e-05)
        return [
            jnp.transpose(jnp.broadcast_to(inv[half : half + 1, :], (LANES, HALF)))
            * jnp.exp2(ke[...].astype(F32))
            for half in range(2)
        ]

    def finish(half, scale):
        total = kown[half]
        for k in range(3):
            wait(kfb.at[half, k], kfb_recv.at[half, k])
            total = total + kfb[half, k].astype(F32)
        rows = rows_of(half)
        ko[rows, :] = (total * scale).astype(BF16)
        pltpu.make_async_copy(ko.at[rows, :], kv_out.at[rows, :], out_sem.at[2 + half]).start()

    wait(rot.at[pl.ds(0, (N - 1) * 16), :], r_recv)

    for i, (dy, dx) in enumerate(ORDER):
        matmul(dy, dx)
        if dx == 2:
            first_far(0, dy)
        if dy == 2:
            first_far(1, dx)
        if i == 6:
            z_start()
        for c in {6: (2,), 10: (1, 3)}.get(i, ()):
            first_near(0, c)
            first_near(1, c)
    for i in range(3, 7):
        loads[i].wait()
    for c in CHUNKS:
        second(0, c)
        second(1, c)
        if c == 2:
            first_near(0, 0)
            first_near(1, 0)
        if c == 3:
            z_finish()
    squares = [residual_rows(0), residual_rows(1)]
    send_squares(*squares)
    wait(wkv.at[pl.ds(0, BLK // 2), :], sib_recv)
    for c in CHUNKS:
        product(c)
        kv_first(0, c)
        if c == 3:
            for k in CHUNKS:
                kv_first(1, k)
    for c in CHUNKS:
        if c == 0:
            scales = row_scales()
        kv_second(0, c)
        kv_second(1, c)
    finish(0, scales[0])
    finish(1, scales[1])

    wait(att.at[pl.ds(0, N - 1)], a_send)
    wait(wkv.at[pl.ds(0, CK), pl.ds(0, (N - 1) * KVB)], k_send)
    wait(turned.at[pl.ds(0, N - 1)], r_send)
    wait(pb.at[pl.ds(0, 3)], p_send)
    wait(pb.at[0, pl.ds(0, 3)], q_send)
    for there, _, _, count in z_sends:

        @pl.when(there)
        def _(count=count):
            wait(wkv.at[pl.ds(0, count), :], z_send)

    wait(wkv.at[pl.ds(0, BLK // 2), :], sib_send)
    wait(sqr.at[pl.ds(0, N - 1)], sq_send)
    wait(pk.at[pl.ds(0, 3)], pk_send)
    wait(pk.at[0, pl.ds(0, 3)], kq_send)
    for half in range(2):
        rows = rows_of(half)
        pltpu.make_async_copy(ro.at[rows, :], resid_out.at[rows, :], out_sem.at[half]).wait()
        pltpu.make_async_copy(ko.at[rows, :], kv_out.at[rows, :], out_sem.at[2 + half]).wait()


def body(attn_out, head_signs, w_out, out_exp, residual, norm_gain, w_kv, kv_exp):
    vmem = pltpu.VMEM
    dma = pltpu.SemaphoreType.DMA
    scratch = [
        pltpu.SMEM((N * LH,), jnp.int32),
        vmem((N, 16, BLK), BF16),
        vmem((N, 16, BLK), F32),
        vmem((N, 16, BLK), BF16),
        vmem((TOK, BLK), BF16),
        vmem((4, 4, BLK, BLK), BF16),
        vmem((4, 4, TOK, BLK), BF16),
        vmem((2, 4, 2, HALF, HCOL), BF16),
        vmem((2, 4, 2, HALF, BLK), BF16),
        vmem((2, 3, HALF, BLK), BF16),
        vmem((2, HALF, BLK), F32),
        vmem((2, 2, HALF, HCOL), BF16),
        vmem((2, 2, HALF, BLK), BF16),
        vmem((BLK, N * KVB), BF16),
        vmem((TOK, BLK), BF16),
        vmem((TOK, BLK), BF16),
        vmem((TOK, BLK), BF16),
        vmem((BLK,), BF16),
        vmem((1, BLK), jnp.int32),
        vmem((1, KVB), jnp.int32),
        vmem((TOK, KVB), BF16),
        vmem((8, LANES), F32),
        vmem((N, 8, LANES), F32),
        vmem((4, 4, TOK, KVB), BF16),
        vmem((2, 4, 3, HALF, KVB), BF16),
        vmem((2, 3, HALF, KVB), BF16),
        vmem((2, HALF, KVB), F32),
        vmem((2, 3, HALF, KVB), BF16),
        dma((7,)),
        dma((16,)),
        dma((4,)),
        dma, dma, dma, dma, dma, dma,
        dma,
        dma((2, 4, 2)),
        dma((2, 4, 2)),
        dma,
        dma((2, 2)),
        dma((2, 2)),
        dma, dma, dma, dma,
        dma, dma,
        dma,
        dma((2, 4, 3)),
        dma,
        dma((2, 3)),
    ]
    anywhere = pl.BlockSpec(memory_space=pl.ANY)
    return pl.pallas_call(
        kernel,
        out_shape=(
            jax.ShapeDtypeStruct((TOK, BLK), BF16),
            jax.ShapeDtypeStruct((TOK, KVB), BF16),
        ),
        in_specs=[anywhere] * 8,
        out_specs=(anywhere, anywhere),
        scratch_shapes=scratch,
        compiler_params=pltpu.CompilerParams(
            collective_id=0, has_side_effects=True, vmem_limit_bytes=62 * 1024 * 1024
        ),
    )(
        attn_out, head_signs, w_out, out_exp.reshape(1, BLK), residual,
        norm_gain, w_kv, kv_exp.reshape(1, KVB),
    )


def solution(mesh):
    placed = (
        P("dp", "tensor"),
        P(),
        P("tensor", None),
        P("tensor"),
        P("dp", "tensor"),
        P("tensor"),
        P(None, "tensor"),
        P("tensor"),
    )
    return jax.shard_map(
        body,
        mesh=mesh,
        in_specs=placed,
        out_specs=(P("dp", "tensor"), P("dp", "tensor")),
        check_vma=False,
    )
```

```python
import jax
import jax.numpy as jnp
from jax import lax
from jax.experimental import pallas as pl
from jax.experimental.pallas import tpu as pltpu
from jax.sharding import PartitionSpec as P

MESH = pl.DeviceIdType.MESH
BF16 = jnp.bfloat16
F32 = jnp.float32
HD = 128
LH = 4
N = 16
TOK = 256
BLK = 512
D = N * BLK
KVB = 128
HALF = TOK // 2
HCOL = BLK // 2
PARTS = 2
PROW = HALF // PARTS
LANES = 128
PLANES = 2
SHARES = 2 * PLANES
CK = BLK // SHARES
PEERS = (
    (2, 2), (2, 1), (1, 2), (2, 3), (3, 2), (2, 0), (0, 2), (1, 1),
    (3, 3), (1, 3), (3, 1), (0, 1), (1, 0), (0, 3), (3, 0),
)
CHUNKS = (2, 1, 3, 0)
ORDER = (
    (2, 2), (1, 2), (2, 1), (3, 2), (2, 3), (0, 2), (2, 0), (1, 1),
    (1, 3), (3, 1), (3, 3), (0, 1), (0, 3), (1, 0), (3, 0), (0, 0),
)


def hadamard(vals):
    step = 1
    while step < len(vals):
        out = list(vals)
        for i in range(len(vals)):
            if not i & step:
                out[i] = vals[i] + vals[i | step]
                out[i | step] = vals[i] - vals[i | step]
        vals = out
        step *= 2
    return vals


def kernel(
    attn, signs, w_out, out_exp, residual, gain, w_kv, kv_exp,
    resid_out, kv_out,
    sgn, lane_signs, att, mixed, turned, rot, w, pb, s1, f, q, s1b, fb,
    wkv, xn, res, ro, gn, oe, ke, ko, sqs, sqr,
    pk, kf, kq, kown, kfb,
    in_sem, w_sem, out_sem,
    a_send, a_recv, k_send, k_recv, r_send, r_recv,
    p_send, s1_recv, f_recv, q_send, s1b_recv, fb_recv,
    z_send, z_recv, sib_send, sib_recv,
    sq_send, sq_recv, pk_send, kf_recv, kq_send, kfb_recv,
):
    me = lax.axis_index("tensor")
    dp = lax.axis_index("dp")
    y, x = me // 4, lax.rem(me, 4)
    z, core = dp // 2, lax.rem(dp, 2)
    nz = lax.axis_size("dp") // 2
    share = core * PLANES + lax.rem(z, PLANES)

    def at_yx(dy, dx):
        return lax.rem(y + dy, 4) * 4 + lax.rem(x + dx, 4)

    along = (
        ({"tensor": at_yx(0, 1)}, {"tensor": at_yx(0, 3)}),
        ({"tensor": at_yx(1, 0)}, {"tensor": at_yx(3, 0)}),
    )

    def at_z(k):
        return {"dp": lax.rem(z + k + nz, nz) * 2 + core}

    top = nz - 1
    z_peers = ((z < top, 1), (z > 0, -1))
    z_sends = (
        (z < top, 1, 0, CK // 2), (z > 0, -1, CK // 2, CK // 2),
        (z == top - 1, 1, CK // 2, CK // 2), (z == 1, -1, 0, CK // 2),
    )
    sibling = {"dp": z * 2 + 1 - core}

    def send(src, dst, send_sem, recv_sem, to):
        pltpu.make_async_remote_copy(
            src_ref=src, dst_ref=dst, send_sem=send_sem, recv_sem=recv_sem,
            device_id=to, device_id_type=MESH,
        ).start()

    def wait(ref, sem):
        pltpu.make_async_copy(ref, ref, sem).wait()

    def to_peers(fn):
        for dy, dx in PEERS:
            fn(at_yx(dy, dx))

    barrier = pltpu.get_barrier_semaphore()

    def greet(j):
        pl.semaphore_signal(barrier, inc=1, device_id={"tensor": j}, device_id_type=MESH)

    to_peers(greet)
    pl.semaphore_signal(barrier, inc=1, device_id=sibling, device_id_type=MESH)
    for there, k in z_peers:

        @pl.when(there)
        def _(k=k):
            pl.semaphore_signal(barrier, inc=1, device_id=at_z(k), device_id_type=MESH)


    mine = pl.ds(pl.multiple_of(me * 16, 16), 16)
    my_rows = pl.ds(pl.multiple_of(share * CK, CK), CK)
    my_cols = pl.ds(pl.multiple_of(me * KVB, KVB), KVB)
    loads = [
        pltpu.make_async_copy(attn.at[mine, :], att.at[me], in_sem.at[0]),
        pltpu.make_async_copy(signs, sgn, in_sem.at[1]),
        pltpu.make_async_copy(
            w_kv.at[pl.ds(pl.multiple_of(me * BLK + share * CK, CK), CK), :],
            wkv.at[my_rows, my_cols], in_sem.at[2],
        ),
        pltpu.make_async_copy(out_exp, oe, in_sem.at[3]),
        pltpu.make_async_copy(residual, res, in_sem.at[4]),
        pltpu.make_async_copy(gain, gn, in_sem.at[5]),
        pltpu.make_async_copy(kv_exp, ke, in_sem.at[6]),
    ]
    for copy in loads:
        copy.start()

    w_loads = {}
    for i, (dy, dx) in enumerate(ORDER):
        columns = pl.ds(pl.multiple_of(at_yx(dy, dx) * BLK, BLK), BLK)
        w_loads[dy, dx] = pltpu.make_async_copy(w_out.at[:, columns], w.at[dy, dx], w_sem.at[i])

    for dy, dx in ORDER:
        w_loads[dy, dx].start()
    pl.semaphore_wait(barrier, N + sum(there.astype(jnp.int32) for there, _ in z_peers))

    def send_tokens(j):
        rows = pl.ds(pl.multiple_of(j * 16, 16), 16)
        send(attn.at[rows, :], att.at[me], a_send, a_recv, {"tensor": j})

    to_peers(send_tokens)

    def send_kv_rows(j, part):
        low = part * (CK // 2)
        rows = pl.ds(pl.multiple_of(j * BLK + share * CK + low, CK // 2), CK // 2)
        slot = pl.ds(pl.multiple_of(share * CK + low, CK // 2), CK // 2)
        send(w_kv.at[rows, :], wkv.at[slot, my_cols], k_send, k_recv, {"tensor": j})

    to_peers(lambda j: send_kv_rows(j, 0))

    loads[1].wait()
    for s in range(N):
        for h in range(LH):
            sign = (2 * sgn[s * LH + h] - 1).astype(F32)
            lane_signs[s : s + 1, h * HD : (h + 1) * HD] = jnp.full((1, HD), sign)
    loads[0].wait()
    wait(att.at[pl.ds(0, N - 1)], a_recv)
    for s in range(N):
        heads = []
        for h in range(LH):
            at = slice(h * HD, (h + 1) * HD)
            heads.append(att[s, :, at].astype(F32) * lane_signs[s : s + 1, at])
        for h, val in enumerate(hadamard(heads)):
            mixed[s, :, h * HD : (h + 1) * HD] = val
    for h in range(LH):
        at = slice(h * HD, (h + 1) * HD)
        for g, val in enumerate(hadamard([mixed[s, :, at] for s in range(N)])):
            turned[g, :, at] = (val * 0.125).astype(BF16)

    def send_turned(j):
        send(turned.at[j], rot.at[mine, :], r_send, r_recv, {"tensor": j})

    to_peers(send_turned)
    to_peers(lambda j: send_kv_rows(j, 1))
    rot[mine, :] = turned[me]

    def z_start():
        loads[2].wait()
        wait(wkv.at[pl.ds(0, CK), pl.ds(0, (N - 1) * KVB)], k_recv)
        for there, k, low, count in z_sends:

            @pl.when(there)
            def _(k=k, low=low, count=count):
                rows = pl.ds(pl.multiple_of(share * CK + low, CK // 2), count)
                send(wkv.at[rows, :], wkv.at[rows, :], z_send, z_recv, at_z(k))

    def z_finish():
        wait(wkv.at[pl.ds(0, (PLANES - 1) * CK), :], z_recv)
        rows = pl.ds(pl.multiple_of(core * (BLK // 2), BLK // 2), BLK // 2)
        send(wkv.at[rows, :], wkv.at[rows, :], sib_send, sib_recv, sibling)

    def block(half, c, a):
        return (c, a) if half == 0 else (a, c)

    def rows_of(half):
        return pl.ds(half * HALF, HALF)

    def matmul(dy, dx):
        w_loads[dy, dx].wait()
        pb[dy, dx] = jnp.dot(rot[...], w[dy, dx], preferred_element_type=F32).astype(BF16)

    def first_far(half, c):
        dy, dx = block(half, c, 2)
        for way in range(2):
            send(
                pb.at[dy, dx, pl.ds(half * HALF, HALF), pl.ds(way * HCOL, HCOL)],
                s1.at[half, c, way], p_send, s1_recv.at[half, c, way], along[half][way],
            )

    def first_near(half, c):
        rows = rows_of(half)
        for way, a in enumerate((1, 3)):
            dy, dx = block(half, c, a)
            part = pl.ds(way * HCOL, HCOL)
            wait(s1.at[half, c, way], s1_recv.at[half, c, way])
            pb[dy, dx, rows, part] = (
                pb[dy, dx, rows, part].astype(F32) + s1[half, c, way].astype(F32)
            ).astype(BF16)
            for p in range(PARTS):
                send(
                    pb.at[dy, dx, pl.ds(half * HALF + p * PROW, PROW), :],
                    f.at[half, c, way, pl.ds(p * PROW, PROW), :],
                    p_send, f_recv.at[half, c, way, p], along[half][way],
                )

    def first_total(half, c, p):
        dy, dx = block(half, c, 0)
        slot = pl.ds(p * PROW, PROW)
        total = pb[dy, dx, pl.ds(half * HALF + p * PROW, PROW), :].astype(F32)
        for way in range(2):
            wait(f.at[half, c, way, slot, :], f_recv.at[half, c, way, p])
            total = total + f[half, c, way, slot, :].astype(F32)
        return total

    def second(half, c, p):
        total = first_total(half, c, p)
        slot = pl.ds(p * PROW, PROW)
        if c == 2:
            q[half, 1, slot, :] = total.astype(BF16)
            for way in range(2):
                send(
                    q.at[half, 1, slot, pl.ds(way * HCOL, HCOL)], s1b.at[half, way, slot, :],
                    q_send, s1b_recv.at[half, way, p], along[1 - half][way],
                )
            return
        way = 0 if c == 1 else 1
        part = slice(way * HCOL, (way + 1) * HCOL)
        rest = slice((1 - way) * HCOL, (2 - way) * HCOL)
        q[half, c - 1, slot, rest] = total[:, rest].astype(BF16)
        wait(s1b.at[half, way, slot, :], s1b_recv.at[half, way, p])
        q[half, c - 1, slot, part] = (total[:, part] + s1b[half, way, slot, :].astype(F32)).astype(BF16)
        send(
            q.at[half, c - 1, slot, :], fb.at[half, way, slot, :],
            q_send, fb_recv.at[half, way, p], along[1 - half][way],
        )

    def residual_rows(half):
        rows = rows_of(half)
        total = jnp.concatenate([first_total(half, 0, p) for p in range(PARTS)], axis=0)
        for way in range(2):
            for p in range(PARTS):
                wait(fb.at[half, way, pl.ds(p * PROW, PROW), :], fb_recv.at[half, way, p])
            total = total + fb[half, way].astype(F32)
        out = (res[rows, :].astype(F32) + total * jnp.exp2(oe[...].astype(F32))).astype(BF16)
        ro[rows, :] = out
        pltpu.make_async_copy(ro.at[rows, :], resid_out.at[rows, :], out_sem.at[half]).start()
        hidden = out.astype(F32)
        xn[rows, :] = (hidden * gn[...].astype(F32).reshape(1, BLK)).astype(BF16)
        column = jnp.sum(hidden * hidden, axis=1, keepdims=True)
        return jnp.transpose(jnp.broadcast_to(column, (HALF, LANES)))[:8, :]

    def send_squares(first_half, second_half):
        index = lax.broadcasted_iota(jnp.int32, (8, LANES), 0)
        sqs[...] = jnp.where(index == 0, first_half, second_half)
        sqr[me] = sqs[...]

        def send_square(j):
            send(sqs, sqr.at[me], sq_send, sq_recv, {"tensor": j})

        to_peers(send_square)

    def product(dy):
        yy = lax.rem(y + dy, 4)
        columns = pl.ds(pl.multiple_of(yy * 4 * KVB, 4 * KVB), 4 * KVB)
        part = jnp.dot(xn[...], wkv[:, columns], preferred_element_type=F32).astype(BF16)
        for k in range(4):
            pk[dy, lax.rem(k + 4 - x, 4)] = part[:, k * KVB : (k + 1) * KVB]

    def kv_first(half, c, a):
        dy, dx = block(half, c, a)
        to = at_yx(0, a) if half == 0 else at_yx(a, 0)
        send(
            pk.at[dy, dx, rows_of(half), :], kf.at[half, c, a - 1],
            pk_send, kf_recv.at[half, c, a - 1], {"tensor": to},
        )

    def kv_second(half, c):
        dy, dx = block(half, c, 0)
        total = pk[dy, dx, rows_of(half), :].astype(F32)
        for k in range(3):
            wait(kf.at[half, c, k], kf_recv.at[half, c, k])
            total = total + kf[half, c, k].astype(F32)
        if c == 0:
            kown[half] = total
            return
        kq[half, c - 1] = total.astype(BF16)
        to = at_yx(c, 0) if half == 0 else at_yx(0, c)
        send(
            kq.at[half, c - 1], kfb.at[half, c - 1],
            kq_send, kfb_recv.at[half, c - 1], {"tensor": to},
        )

    def row_scales():
        wait(sqr.at[pl.ds(0, N - 1)], sq_recv)
        total_sq = sqr[0]
        for s in range(1, N):
            total_sq = total_sq + sqr[s]
        inv = lax.rsqrt(total_sq / D + 1e-05)
        return [
            jnp.transpose(jnp.broadcast_to(inv[half : half + 1, :], (LANES, HALF)))
            * jnp.exp2(ke[...].astype(F32))
            for half in range(2)
        ]

    def finish(half, scale):
        total = kown[half]
        for k in range(3):
            wait(kfb.at[half, k], kfb_recv.at[half, k])
            total = total + kfb[half, k].astype(F32)
        rows = rows_of(half)
        ko[rows, :] = (total * scale).astype(BF16)
        pltpu.make_async_copy(ko.at[rows, :], kv_out.at[rows, :], out_sem.at[2 + half]).start()

    wait(rot.at[pl.ds(0, (N - 1) * 16), :], r_recv)

    for i, (dy, dx) in enumerate(ORDER):
        matmul(dy, dx)
        if dx == 2:
            first_far(0, dy)
        if dy == 2:
            first_far(1, dx)
        if i == 6:
            z_start()
        for c in {6: (2,), 10: (1, 3)}.get(i, ()):
            first_near(0, c)
            first_near(1, c)
    for i in range(3, 7):
        loads[i].wait()
    for c in CHUNKS[:3]:
        for p in range(PARTS):
            second(0, c, p)
            second(1, c, p)
        if c == 2:
            first_near(0, 0)
            first_near(1, 0)
        if c == 3:
            z_finish()
    squares = [residual_rows(0), residual_rows(1)]
    wait(wkv.at[pl.ds(0, BLK // 2), :], sib_recv)
    for d in CHUNKS:
        product(d)
        for a in (2, 1, 3):
            kv_first(0, d, a)
        if d:
            for c in CHUNKS:
                kv_first(1, c, d)
    send_squares(*squares)
    for c in CHUNKS:
        if c == 0:
            scales = row_scales()
        kv_second(0, c)
        kv_second(1, c)
    finish(0, scales[0])
    finish(1, scales[1])

    wait(att.at[pl.ds(0, N - 1)], a_send)
    wait(wkv.at[pl.ds(0, CK), pl.ds(0, (N - 1) * KVB)], k_send)
    wait(turned.at[pl.ds(0, N - 1)], r_send)
    wait(pb.at[pl.ds(0, 3)], p_send)
    wait(pb.at[0, pl.ds(0, 3)], q_send)
    for there, _, _, count in z_sends:

        @pl.when(there)
        def _(count=count):
            wait(wkv.at[pl.ds(0, count), :], z_send)

    wait(wkv.at[pl.ds(0, BLK // 2), :], sib_send)
    wait(sqr.at[pl.ds(0, N - 1)], sq_send)
    wait(pk.at[pl.ds(0, 3)], pk_send)
    wait(pk.at[0, pl.ds(0, 3)], kq_send)
    for half in range(2):
        rows = rows_of(half)
        pltpu.make_async_copy(ro.at[rows, :], resid_out.at[rows, :], out_sem.at[half]).wait()
        pltpu.make_async_copy(ko.at[rows, :], kv_out.at[rows, :], out_sem.at[2 + half]).wait()


def body(attn_out, head_signs, w_out, out_exp, residual, norm_gain, w_kv, kv_exp):
    vmem = pltpu.VMEM
    dma = pltpu.SemaphoreType.DMA
    scratch = [
        pltpu.SMEM((N * LH,), jnp.int32),
        vmem((N, BLK), F32),
        vmem((N, 16, BLK), BF16),
        vmem((N, 16, BLK), F32),
        vmem((N, 16, BLK), BF16),
        vmem((TOK, BLK), BF16),
        vmem((4, 4, BLK, BLK), BF16),
        vmem((4, 4, TOK, BLK), BF16),
        vmem((2, 4, 2, HALF, HCOL), BF16),
        vmem((2, 4, 2, HALF, BLK), BF16),
        vmem((2, 3, HALF, BLK), BF16),
        vmem((2, 2, HALF, HCOL), BF16),
        vmem((2, 2, HALF, BLK), BF16),
        vmem((BLK, N * KVB), BF16),
        vmem((TOK, BLK), BF16),
        vmem((TOK, BLK), BF16),
        vmem((TOK, BLK), BF16),
        vmem((BLK,), BF16),
        vmem((1, BLK), jnp.int32),
        vmem((1, KVB), jnp.int32),
        vmem((TOK, KVB), BF16),
        vmem((8, LANES), F32),
        vmem((N, 8, LANES), F32),
        vmem((4, 4, TOK, KVB), BF16),
        vmem((2, 4, 3, HALF, KVB), BF16),
        vmem((2, 3, HALF, KVB), BF16),
        vmem((2, HALF, KVB), F32),
        vmem((2, 3, HALF, KVB), BF16),
        dma((7,)),
        dma((16,)),
        dma((4,)),
        dma, dma, dma, dma, dma, dma,
        dma,
        dma((2, 4, 2)),
        dma((2, 4, 2, PARTS)),
        dma,
        dma((2, 2, PARTS)),
        dma((2, 2, PARTS)),
        dma, dma, dma, dma,
        dma, dma,
        dma,
        dma((2, 4, 3)),
        dma,
        dma((2, 3)),
    ]
    anywhere = pl.BlockSpec(memory_space=pl.ANY)
    return pl.pallas_call(
        kernel,
        out_shape=(
            jax.ShapeDtypeStruct((TOK, BLK), BF16),
            jax.ShapeDtypeStruct((TOK, KVB), BF16),
        ),
        in_specs=[anywhere] * 8,
        out_specs=(anywhere, anywhere),
        scratch_shapes=scratch,
        compiler_params=pltpu.CompilerParams(
            collective_id=0, has_side_effects=True, vmem_limit_bytes=62 * 1024 * 1024
        ),
    )(
        attn_out, head_signs, w_out, out_exp.reshape(1, BLK), residual,
        norm_gain, w_kv, kv_exp.reshape(1, KVB),
    )


def solution(mesh):
    placed = (
        P("dp", "tensor"),
        P(),
        P("tensor", None),
        P("tensor"),
        P("dp", "tensor"),
        P("tensor"),
        P(None, "tensor"),
        P("tensor"),
    )
    return jax.shard_map(
        body,
        mesh=mesh,
        in_specs=placed,
        out_specs=(P("dp", "tensor"), P("dp", "tensor")),
        check_vma=False,
    )
```
